256 devices in a mesh: grp: 16 (over x_hi, y, core), sub: 16 (over x_lo, z).
Axes of the slice: x: 4 (x_hi: 2, x_lo: 2; x = x_hi * 2 + x_lo), y: 4, z: 8, core: 2. Of those that a mesh axis runs over, the one named last changes fastest.
Arguments:
- operator_fine: bfloat16 [8192, 96, 480], P(('grp', 'sub')), may hold values from -1 to 1
- rhs_fine: bfloat16 [8192, 96, 128], P(('grp', 'sub')), may hold values from -13 to 13
- fine_site: int32 [8192], P('grp'), may hold values from 0 to 8191, as said below
Outputs:
- solution: float32 [8192, 96, 128], P(('grp', 'sub'))
- residual: float32 [8192, 96, 128], P(('grp', 'sub'))
The draws below stay inside these ranges and needn't reach their ends.
Inputs may be any that keep to these rules, and one draw needn't show every extreme that they name: `fine_site`: A permutation of the coarse sites. The 32 fine rows of one device name only coarse sites of the devices of its own grp group, the same number of them for each device of that group.
All inputs are finite; a program needn't handle non-finite values.
Results may differ from the reference program's by a relative error of at most 0.015.
Values may be sent and summed in bfloat16 or wider, within the bound.
A program may use at most 128 MiB of HBM per device.

```python
import jax
import jax.numpy as jnp
from jax import lax

BLK = 96
RHS = 128
STEPS = 4
LX = 8
LY = 4
LZ = 1
LT = 1
SITE_DEV = 32
NY = 8
NZ = 8
NT = 16
SITES = 8192
N_GRP = 16
N_SUB = 16


def site_table(key):
    all_devices = N_GRP * N_SUB
    share = SITE_DEV // N_SUB
    key_orders, key_offsets, key_mixing = jax.random.split(jax.random.fold_in(key, 7), 3)
    owner_orders = jax.vmap(lambda one_key: jax.random.permutation(one_key, SITE_DEV))(jax.random.split(key_orders, all_devices))
    offsets = jax.random.randint(key_offsets, (all_devices,), 0, N_SUB)
    group_ids = jnp.arange(N_GRP)[:, None, None]
    fine_ids = jnp.arange(N_SUB)[None, :, None]
    other_ids = jnp.arange(N_SUB)[None, None, :]
    owner_ids = jnp.broadcast_to(group_ids * N_SUB + other_ids, (N_GRP, N_SUB, N_SUB))
    pieces = (fine_ids + offsets[owner_ids]) % N_SUB
    slot_ids = pieces[..., None] * share + jnp.arange(share)
    local_ids = owner_orders[owner_ids[..., None], slot_ids]
    coarse_ids = (owner_ids[..., None] * SITE_DEV + local_ids).reshape(all_devices, SITE_DEV)
    mixing = jax.vmap(lambda one_key: jax.random.permutation(one_key, SITE_DEV))(jax.random.split(key_mixing, all_devices))
    return jnp.take_along_axis(coarse_ids, mixing, axis=1).reshape(all_devices * SITE_DEV).astype(jnp.int32)


def time_share(coarse_ids):
    device = coarse_ids // SITE_DEV
    layer = coarse_ids % SITE_DEV // (LZ * LY * LX)
    time_index = device // N_SUB * LT + layer
    return time_index.astype(jnp.float32) / max(NT - 1, 1)


def draw_fine_site(key, part):
    return site_table(key)


def draw_operator_fine(key, part):
    coarse_ids = site_table(key)
    rising = time_share(coarse_ids)
    noise_key = jax.random.fold_in(key, 13)
    strength = 0.25 + 0.75 * rising
    values = jnp.clip(jax.random.normal(noise_key, (SITES, BLK, 5 * BLK), jnp.float32), -4.0, 4.0)
    scale = (strength * BLK ** (-0.5))[:, None, None]
    return (values * scale).astype(jnp.bfloat16)


def draw_rhs_fine(key, part):
    coarse_ids = site_table(key)
    device = coarse_ids // SITE_DEV
    within = coarse_ids % SITE_DEV
    layer = within // (LZ * LY * LX)
    slab_ids = within // (LY * LX) % LZ
    time_index = device // N_SUB * LT + layer
    depth_index = device % N_SUB // 2 * LZ + slab_ids
    rise_time = 0.6 + 1.2 * time_index.astype(jnp.float32) / max(NT - 1, 1)
    rise_depth = 0.6 + 1.2 * depth_index.astype(jnp.float32) / max(NZ - 1, 1)
    scale = (rise_time * rise_depth)[:, None, None]
    noise_key = jax.random.fold_in(key, 11)
    values = jnp.clip(jax.random.normal(noise_key, (SITES, BLK, RHS), jnp.float32), -4.0, 4.0)
    return (values * scale).astype(jnp.bfloat16)


def setup_inputs(seed: int = 0) -> dict:
    key_list = jax.random.split(jax.random.key(seed), 4)
    return {
        "operator_fine": draw_operator_fine(jax.random.fold_in(key_list[3], 71), 0),
        "rhs_fine": draw_rhs_fine(jax.random.fold_in(key_list[3], 71), 0),
        "fine_site": draw_fine_site(jax.random.fold_in(key_list[3], 71), 0),
    }


def chirality(width):
    return jnp.where(jnp.arange(width) < width // 2, 1.0, -1.0).astype(jnp.float32)


def to_lattice(flat):
    tail = flat.shape[1:]
    extra = tuple(range(7, 7 + len(tail)))
    shaped = flat.reshape((N_GRP, N_SUB // 2, 2, LT, LZ, LY, LX) + tail)
    shaped = jnp.transpose(shaped, (0, 3, 1, 4, 2, 5, 6) + extra)
    return shaped.reshape((NT, NZ, NY, LX) + tail)


def from_lattice(field):
    tail = field.shape[4:]
    extra = tuple(range(7, 7 + len(tail)))
    shaped = field.reshape((N_GRP, LT, N_SUB // 2, LZ, 2, LY, LX) + tail)
    shaped = jnp.transpose(shaped, (0, 2, 4, 1, 3, 5, 6) + extra)
    return shaped.reshape((SITES,) + tail)


def operate(rounded, blocks):
    vector = rounded.astype(jnp.float32)
    sign = chirality(BLK)[:, None]
    image = 4.0 * vector + jnp.einsum("abcdij,abcdjr->abcdir", blocks[..., :BLK].astype(jnp.float32), vector, precision=lax.Precision.HIGHEST)
    for hop, axis in zip(range(1, 5), (3, 2, 1, 0)):
        block = blocks[..., hop * BLK:(hop + 1) * BLK].astype(jnp.float32)
        image = image + jnp.einsum("abcdij,abcdjr->abcdir", block, jnp.roll(vector, -1, axis), precision=lax.Precision.HIGHEST)
        behind = jnp.einsum("abcdij,abcdir->abcdjr", block, vector * sign, precision=lax.Precision.HIGHEST) * sign
        image = image + jnp.roll(behind, 1, axis)
    return image


def reference(operator_fine, rhs_fine, fine_site):
    inverse = jnp.argsort(fine_site)
    blocks = to_lattice(operator_fine[inverse])
    source = to_lattice(rhs_fine[inverse])
    residual = source.astype(jnp.float32)
    solution = jnp.zeros(residual.shape, jnp.float32)
    for step in range(STEPS):
        rounded = residual.astype(jnp.bfloat16)
        image = operate(rounded, blocks)
        cross = jnp.sum(image * residual, axis=(0, 1, 2, 3, 4))
        power = jnp.sum(image * image, axis=(0, 1, 2, 3, 4))
        alpha = cross / power
        solution = solution + alpha * rounded.astype(jnp.float32)
        residual = residual - alpha * image
    return from_lattice(solution), from_lattice(residual)
```

```python
import jax
import jax.numpy as jnp
from jax import lax
from jax.experimental import pallas as pl
from jax.experimental.pallas import tpu as pltpu
from jax.sharding import PartitionSpec as P

MESH = pl.DeviceIdType.MESH
STEPS = 4
LX = 8
LY = 4
SITES = 32
BLK = 96
RHS = 128
N_GRP = 16
N_SUB = 16
CUT = 256
WIDE = 5 * BLK


def place(logical):
    return logical


def logical_of(position):
    return position


def tables(fine_site):
    position = lax.axis_index("sub")
    sites = fine_site.reshape(N_SUB, SITES)
    target = place(sites // SITES % N_SUB)
    before = jnp.arange(SITES)[:, None] > jnp.arange(SITES)[None, :]
    here = (jnp.arange(N_SUB) == position)[:, None]
    mine = jnp.sum(jnp.where(here, target, 0), axis=0)
    rank = jnp.sum((mine[:, None] == mine[None, :]) & before, axis=1)
    slot = 2 * mine + rank
    order = jnp.sum(
        jnp.where(slot[None, :] == jnp.arange(SITES)[:, None], jnp.arange(SITES)[None, :], 0), axis=1
    )
    hit = target == position
    arrival = jnp.sum(hit[:, None, :] & before[None], axis=2) + 2 * jnp.arange(N_SUB)[:, None]
    match = hit[None] & ((sites % SITES)[None] == jnp.arange(SITES)[:, None, None])
    inverse = jnp.sum(jnp.where(match, arrival[None], 0), axis=(1, 2))
    return order.astype(jnp.int32), inverse.astype(jnp.int32)


def kernel(
    order, inverse, op, rhs, sol, res,
    send_op, send_rhs, got_op, got_rhs, flipped, v, vz, vt, zs, ts, ys, bz, bt, by, bx, byl, image,
    alpha, sums, rows, cols,
    op_send, op_recv, rhs_send, rhs_recv, halo_send, halo_recv, y_send, y_recv, sum_send, sum_recv,
):
    f32, bf16 = jnp.float32, jnp.bfloat16
    grp = lax.axis_index("grp")
    sub = lax.axis_index("sub")

    def along_sub(d):
        return lax.rem(sub + d + N_SUB, N_SUB)

    def along_grp(d):
        return lax.rem(grp + d + N_GRP, N_GRP)

    barrier = pltpu.get_barrier_semaphore()

    def greet(d, _):
        pl.semaphore_signal(barrier, inc=1, device_id={"sub": along_sub(d)}, device_id_type=MESH)
        pl.semaphore_signal(barrier, inc=1, device_id={"grp": along_grp(d)}, device_id_type=MESH)
        return 0

    lax.fori_loop(1, 16, greet, 0)
    pl.semaphore_wait(barrier, 30)

    def row_copy(d, to, who, buf, got, send, recv):
        return pltpu.make_async_remote_copy(
            src_ref=buf.at[pl.ds(2 * to, 2)], dst_ref=got.at[pl.ds(2 * who, 2)],
            send_sem=send.at[d], recv_sem=recv.at[d], device_id={"sub": to}, device_id_type=MESH,
        )

    def send_vectors(d, _):
        to = along_sub(d)
        for k in range(2):
            send_rhs[2 * to + k] = rhs[order[2 * to + k]]
        row_copy(d, to, sub, send_rhs, got_rhs, rhs_send, rhs_recv).start()
        return 0

    lax.fori_loop(1, 16, send_vectors, 0)

    def send_blocks(d, _):
        to = along_sub(d)
        for k in range(2):
            send_op[2 * to + k] = op[order[2 * to + k]]
        row_copy(d, to, sub, send_op, got_op, op_send, op_recv).start()
        return 0

    lax.fori_loop(1, 16, send_blocks, 0)
    for k in range(2):
        got_rhs[2 * sub + k] = rhs[order[2 * sub + k]]
        got_op[2 * sub + k] = op[order[2 * sub + k]]

    sign_row = jnp.where(lax.broadcasted_iota(jnp.int32, (BLK, 1), 0) < BLK // 2, 1.0, -1.0).astype(f32)
    lane = lax.broadcasted_iota(jnp.int32, (1, WIDE), 1)
    sign_lane = jnp.where(lax.rem(lane, BLK) < BLK // 2, 1.0, -1.0).astype(f32)

    def flip(who):
        for k in range(2):
            signed = got_op[2 * who + k].astype(f32) * sign_row * sign_lane
            turned = jnp.transpose(signed)
            flipped[2 * who + k] = turned[BLK:].astype(bf16)

    flip(sub)

    def take_vectors(d, _):
        row_copy(d, along_sub(d), along_sub(-d), send_rhs, got_rhs, rhs_send, rhs_recv).wait()
        return 0

    lax.fori_loop(1, 16, take_vectors, 0)

    def begin(l, _):
        start = got_rhs[inverse[l]].astype(f32)
        res[l] = start
        sol[l] = jnp.zeros_like(start)
        image[l] = jnp.zeros_like(start)
        return 0

    lax.fori_loop(0, SITES, begin, 0)
    alpha[...] = jnp.zeros_like(alpha)

    def take_blocks(d, _):
        who = along_sub(-d)
        row_copy(d, along_sub(d), who, send_op, got_op, op_send, op_recv).wait()
        flip(who)
        return 0

    lax.fori_loop(1, 16, take_blocks, 0)

    here = logical_of(sub)
    half, layer = lax.rem(here, 2), here // 2
    other = place(2 * layer + 1 - half)
    z_down = place(2 * lax.rem(layer + 7, 8) + half)
    z_up = place(2 * lax.rem(layer + 1, 8) + half)
    t_down, t_up = along_grp(-1), along_grp(1)

    def halo(step, kind, chunk):
        part = pl.ds(LX * chunk, LX)
        src, dst, to = (
            (v.at[step, part], vz.at[step, part], {"sub": z_down}),
            (v.at[step, part], vt.at[step, part], {"grp": t_down}),
            (zs.at[step, part], bz.at[step, part], {"sub": z_up}),
            (ts.at[step, part], bt.at[step, part], {"grp": t_up}),
        )[kind]
        return pltpu.make_async_remote_copy(
            src_ref=src, dst_ref=dst, send_sem=halo_send.at[step, kind, chunk],
            recv_sem=halo_recv.at[step, kind, chunk], device_id=to, device_id_type=MESH,
        )

    def y_halo(step, kind):
        src, dst = (
            (v.at[step, pl.ds(0, LX)], v.at[step, pl.ds(SITES, LX)]),
            (ys.at[step], by.at[step]),
        )[kind]
        return pltpu.make_async_remote_copy(
            src_ref=src, dst_ref=dst, send_sem=y_send.at[step, kind],
            recv_sem=y_recv.at[step, kind], device_id={"sub": other}, device_id_type=MESH,
        )

    def sum_copy(step, stage, d):
        to, buf = ({"sub": along_sub(d)}, rows) if stage == 0 else ({"grp": along_grp(d)}, cols)
        return pltpu.make_async_remote_copy(
            src_ref=buf.at[step, 0], dst_ref=buf.at[step, d], send_sem=sum_send.at[step, stage, d],
            recv_sem=sum_recv.at[step, stage, d], device_id=to, device_id_type=MESH,
        )

    def one_step(step, _):
        def update(l, _):
            new = res[l] - alpha[...] * image[l]
            res[l] = new
            v[step, l] = new.astype(bf16)
            return 0

        def behind(l, _):
            terms = jnp.dot(flipped[inverse[l]], v[step, l], preferred_element_type=f32)
            bx[l] = terms[:BLK]
            byl[l] = terms[BLK : 2 * BLK]
            zs[step, l] = terms[2 * BLK : 3 * BLK].astype(bf16)
            ts[step, l] = terms[3 * BLK :].astype(bf16)
            return 0

        for chunk in range(LY):
            lax.fori_loop(LX * chunk, LX * chunk + LX, update, 0)
            halo(step, 0, chunk).start()
            halo(step, 1, chunk).start()
            if chunk == 0:
                y_halo(step, 0).start()
            lax.fori_loop(LX * chunk, LX * chunk + LX, behind, 0)
            halo(step, 2, chunk).start()
            halo(step, 3, chunk).start()

        def pack(x, _):
            ys[step, x] = byl[SITES - LX + x].astype(bf16)
            return 0

        lax.fori_loop(0, LX, pack, 0)
        y_halo(step, 1).start()

        def near(l, back):
            row = l // LX * LX
            x = l - row
            ahead = row + lax.rem(x + 1, LX)
            behind_x = row + lax.rem(x + LX - 1, LX)
            this = v[step, l]
            stack = jnp.concatenate([this, v[step, ahead], v[step, l + LX, : CUT - 2 * BLK]], axis=0)
            total = jnp.dot(got_op[inverse[l], :, :CUT], stack, preferred_element_type=f32)
            image[l] = total + 4.0 * this.astype(f32) + bx[behind_x] + back

        def near_inner(l, _):
            near(l, byl[l - LX])
            return 0

        def near_first(l, _):
            near(l, by[step, l].astype(f32))
            return 0

        lax.fori_loop(LX, SITES - LX, near_inner, 0)
        y_halo(step, 0).wait()
        lax.fori_loop(SITES - LX, SITES, near_inner, 0)
        y_halo(step, 1).wait()
        lax.fori_loop(0, LX, near_first, 0)

        def far(l, carry):
            cross, power = carry
            stack = jnp.concatenate(
                [v[step, l + LX, CUT - 2 * BLK :], vz[step, l], vt[step, l]], axis=0
            )
            total = jnp.dot(got_op[inverse[l], :, CUT:], stack, preferred_element_type=f32)
            total = total + image[l] + bz[step, l].astype(f32) + bt[step, l].astype(f32)
            image[l] = total
            old = res[l]
            cross = cross + jnp.sum((total * old).reshape(BLK // 8, 8, RHS), axis=0)
            power = power + jnp.sum((total * total).reshape(BLK // 8, 8, RHS), axis=0)
            return cross, power

        carry = (jnp.zeros((8, RHS), f32), jnp.zeros((8, RHS), f32))
        for chunk in range(LY):
            for kind in range(4):
                halo(step, kind, chunk).wait()
            carry = lax.fori_loop(LX * chunk, LX * chunk + LX, far, carry)
        both = jnp.concatenate([jnp.sum(c, axis=0, keepdims=True) for c in carry] + [jnp.zeros((6, RHS), f32)], axis=0)
        for stage, buf in enumerate((rows, cols)):
            buf[step, 0] = both

            def start(d, _):
                sum_copy(step, stage, d).start()
                return 0

            def finish(d, _):
                sum_copy(step, stage, d).wait()
                return 0

            lax.fori_loop(1, 16, start, 0)
            lax.fori_loop(1, 16, finish, 0)
            both = jnp.sum(buf[step], axis=0)
        alpha[...] = both[0:1] / both[1:2]

        def grow(l, _):
            sol[l] = sol[l] + alpha[...] * v[step, l].astype(f32)
            return 0

        lax.fori_loop(0, SITES, grow, 0)
        return 0

    lax.fori_loop(0, STEPS, one_step, 0)

    def last(l, _):
        res[l] = res[l] - alpha[...] * image[l]
        return 0

    lax.fori_loop(0, SITES, last, 0)


def on_device(operator_fine, rhs_fine, fine_site):
    f32, bf16 = jnp.float32, jnp.bfloat16
    order, inverse = tables(fine_site)
    vector = (SITES, BLK, RHS)
    whole = pl.BlockSpec(memory_space=pltpu.VMEM)
    scalars = pl.BlockSpec(memory_space=pltpu.SMEM)
    dma = pltpu.SemaphoreType.DMA
    return pl.pallas_call(
        kernel,
        out_shape=(jax.ShapeDtypeStruct(vector, f32), jax.ShapeDtypeStruct(vector, f32)),
        in_specs=[scalars, scalars, whole, whole],
        out_specs=(whole, whole),
        scratch_shapes=[
            pltpu.VMEM((SITES, BLK, WIDE), bf16),
            pltpu.VMEM(vector, bf16),
            pltpu.VMEM((SITES, BLK, WIDE), bf16),
            pltpu.VMEM(vector, bf16),
            pltpu.VMEM((SITES, 4 * BLK, BLK), bf16),
            pltpu.VMEM((STEPS, SITES + LX, BLK, RHS), bf16),
            pltpu.VMEM((STEPS,) + vector, bf16),
            pltpu.VMEM((STEPS,) + vector, bf16),
            pltpu.VMEM((STEPS,) + vector, bf16),
            pltpu.VMEM((STEPS,) + vector, bf16),
            pltpu.VMEM((STEPS, LX, BLK, RHS), bf16),
            pltpu.VMEM((STEPS,) + vector, bf16),
            pltpu.VMEM((STEPS,) + vector, bf16),
            pltpu.VMEM((STEPS, LX, BLK, RHS), bf16),
            pltpu.VMEM(vector, f32),
            pltpu.VMEM(vector, f32),
            pltpu.VMEM(vector, f32),
            pltpu.VMEM((1, RHS), f32),
            pltpu.VMEM((8, RHS), f32),
            pltpu.VMEM((STEPS, 16, 8, RHS), f32),
            pltpu.VMEM((STEPS, 16, 8, RHS), f32),
            dma((16,)), dma((16,)), dma((16,)), dma((16,)),
            dma((STEPS, 4, LY)), dma((STEPS, 4, LY)),
            dma((STEPS, 2)), dma((STEPS, 2)),
            dma((STEPS, 2, 16)), dma((STEPS, 2, 16)),
        ],
        compiler_params=pltpu.CompilerParams(
            collective_id=0, has_side_effects=True, vmem_limit_bytes=60 * 2**20
        ),
    )(order, inverse, operator_fine, rhs_fine)


def solution(mesh):
    in_specs = (P(("grp", "sub"), None, None), P(("grp", "sub"), None, None), P("grp"))
    out_specs = (P(("grp", "sub"), None, None), P(("grp", "sub"), None, None))
    return jax.shard_map(
        on_device, mesh=mesh, in_specs=in_specs, out_specs=out_specs, check_vma=False
    )
```

```python
import jax
import jax.numpy as jnp
from jax import lax
from jax.experimental import pallas as pl
from jax.experimental.pallas import tpu as pltpu
from jax.sharding import PartitionSpec as P

MESH = pl.DeviceIdType.MESH
STEPS = 4
LX = 8
LY = 4
SITES = 32
BLK = 96
RHS = 128
N_GRP = 16
N_SUB = 16
GUESS = 0.25
CUT = 256
WIDE = 5 * BLK


def place(logical):
    return logical % 2 * 8 + (8 - logical // 2) % 8


def logical_of(position):
    return (8 - position % 8) % 8 * 2 + position // 8


def tables(fine_site, sub):
    i32 = jnp.int32
    iota = lax.broadcasted_iota
    spread = jnp.concatenate([jnp.broadcast_to(fine_site[k : k + 1], (4, 128)) for k in range(4)], axis=0)
    device, lane = iota(i32, (N_SUB, 128), 0), iota(i32, (N_SUB, 128), 1)
    valid = lane // SITES == device % 4
    target = jnp.where(valid, place(spread // SITES % N_SUB), -1)
    mine = jnp.sum(jnp.where(device == sub, target + 1, 0), axis=0, keepdims=True) - 1
    down, across = iota(i32, (128, 128), 0), iota(i32, (128, 128), 1)
    column = jnp.sum(jnp.where(down == across, jnp.broadcast_to(mine, (128, 128)), 0), axis=1, keepdims=True)
    rank = jnp.sum(jnp.where((column == mine) & (across < down), 1, 0), axis=1, keepdims=True)
    slot = jnp.where(column >= 0, 2 * column + rank, -1)
    order = jnp.sum(jnp.where(slot == across, down % SITES, 0), axis=0, keepdims=True)
    hit = target == sub
    second = jnp.max(jnp.where(hit, lane, -1), axis=1, keepdims=True)
    site = spread % SITES
    site_b = jnp.sum(jnp.where(hit & (lane == second), site, 0), axis=1, keepdims=True)
    site_a = jnp.sum(jnp.where(hit & (lane < second), site, 0), axis=1, keepdims=True)
    inverse = jnp.sum(
        jnp.where(site_a == lane, 2 * device, 0) + jnp.where(site_b == lane, 2 * device + 1, 0), axis=0, keepdims=True
    )
    return jnp.minimum(jnp.concatenate([order, inverse], axis=0), SITES - 1)


def kernel(
    fine, op_hbm, rhs_hbm, sol_out, res_out,
    op, rhs, listed, table, send_op, send_rhs, got_op, got_rhs, flipped,
    u, uz, ut, uy, zs, ts, ys, bz, bt, by, v, bx, byl, image, halo_sum, sol, res, home,
    alpha, rows, cols,
    op_send, op_recv, rhs_send, rhs_recv, halo_send, halo_recv, y_send, y_recv, sum_send, sum_recv, home_send, home_recv, local_sem,
):
    f32, bf16 = jnp.float32, jnp.bfloat16
    grp = lax.axis_index("grp")
    sub = lax.axis_index("sub")

    def along_sub(d):
        return lax.rem(sub + d + N_SUB, N_SUB)

    def along_grp(d):
        return lax.rem(grp + d + N_GRP, N_GRP)

    load_rhs = pltpu.make_async_copy(rhs_hbm, rhs, local_sem.at[0])
    load_op = pltpu.make_async_copy(op_hbm, op, local_sem.at[1])
    load_rhs.start()
    load_op.start()
    barrier = pltpu.get_barrier_semaphore()

    def greet(d, _):
        pl.semaphore_signal(barrier, inc=1, device_id={"sub": along_sub(d)}, device_id_type=MESH)
        pl.semaphore_signal(barrier, inc=1, device_id={"grp": along_grp(d)}, device_id_type=MESH)
        return 0

    lax.fori_loop(1, 16, greet, 0)

    def row_copy(d, to, who, buf, got, send, recv):
        return pltpu.make_async_remote_copy(
            src_ref=buf.at[pl.ds(2 * to, 2)], dst_ref=got.at[pl.ds(2 * who, 2)],
            send_sem=send.at[d], recv_sem=recv.at[d], device_id={"sub": to}, device_id_type=MESH,
        )

    listed[...] = tables(fine[...], sub)
    to_scalars = pltpu.make_async_copy(listed, table, local_sem.at[2])
    to_scalars.start()
    to_scalars.wait()
    load_rhs.wait()

    def pack_vectors(j, _):
        send_rhs[j] = rhs[table[0, j]]
        return 0

    lax.fori_loop(0, SITES, pack_vectors, 0, unroll=4)
    pl.semaphore_wait(barrier, 30)

    def send_vectors(d, _):
        to = along_sub(d)
        row_copy(d, to, sub, send_rhs, got_rhs, rhs_send, rhs_recv).start()
        return 0

    lax.fori_loop(1, 16, send_vectors, 0)
    load_op.wait()

    def send_blocks(d, _):
        to = along_sub(d)
        for k in range(2):
            send_op[2 * to + k] = op[table[0, 2 * to + k]]
        row_copy(d, to, sub, send_op, got_op, op_send, op_recv).start()
        return 0

    lax.fori_loop(1, 16, send_blocks, 0)
    for k in range(2):
        got_rhs[2 * sub + k] = rhs[table[0, 2 * sub + k]]
        got_op[2 * sub + k] = op[table[0, 2 * sub + k]]

    sign_row = jnp.where(lax.broadcasted_iota(jnp.int32, (BLK, 1), 0) < BLK // 2, 1.0, -1.0).astype(f32)
    lane = lax.broadcasted_iota(jnp.int32, (1, WIDE), 1)
    sign_lane = jnp.where(lax.rem(lane, BLK) < BLK // 2, 1.0, -1.0).astype(f32)

    def flip(who):
        for k in range(2):
            signed = got_op[2 * who + k].astype(f32) * sign_row * sign_lane
            turned = jnp.transpose(signed)
            flipped[2 * who + k] = turned[BLK:].astype(bf16)

    flip(sub)

    def take_vectors(d, _):
        row_copy(d, along_sub(d), along_sub(-d), send_rhs, got_rhs, rhs_send, rhs_recv).wait()
        return 0

    lax.fori_loop(1, 16, take_vectors, 0)

    here = logical_of(sub)
    half, layer = lax.rem(here, 2), here // 2
    other = place(2 * layer + 1 - half)
    z_down = place(2 * lax.rem(layer + 7, 8) + half)
    z_up = place(2 * lax.rem(layer + 1, 8) + half)
    t_down, t_up = along_grp(-1), along_grp(1)

    def halo(step, kind, chunk):
        part = pl.ds(LX * chunk, LX)
        src, dst, to = (
            (u.at[part], uz.at[step, part], {"sub": z_down}),
            (u.at[part], ut.at[step, part], {"grp": t_down}),
            (zs.at[part], bz.at[step, part], {"sub": z_up}),
            (ts.at[part], bt.at[step, part], {"grp": t_up}),
        )[kind]
        return pltpu.make_async_remote_copy(
            src_ref=src, dst_ref=dst, send_sem=halo_send.at[step, kind, chunk],
            recv_sem=halo_recv.at[step, kind, chunk], device_id=to, device_id_type=MESH,
        )

    def y_halo(step, kind):
        src, dst = (
            (u.at[pl.ds(0, LX)], uy.at[step]),
            (ys, by.at[step]),
        )[kind]
        return pltpu.make_async_remote_copy(
            src_ref=src, dst_ref=dst, send_sem=y_send.at[step, kind],
            recv_sem=y_recv.at[step, kind], device_id={"sub": other}, device_id_type=MESH,
        )

    def sum_copy(step, stage, d):
        to, buf = ({"sub": along_sub(d)}, rows) if stage == 0 else ({"grp": along_grp(d)}, cols)
        return pltpu.make_async_remote_copy(
            src_ref=buf.at[step, 0], dst_ref=buf.at[step, d], send_sem=sum_send.at[step, stage],
            recv_sem=sum_recv.at[step, stage], device_id=to, device_id_type=MESH,
        )

    def begin(l, _):
        start = got_rhs[table[1, l]]
        u[l] = start
        image[l] = start.astype(f32) * (-1.0 / GUESS)
        v[l] = jnp.zeros_like(start)
        res[l] = jnp.zeros((BLK, RHS), f32)
        sol[l] = jnp.zeros((BLK, RHS), f32)
        halo_sum[l] = jnp.zeros((BLK, RHS), f32)
        return 0

    def take_blocks(d, _):
        who = along_sub(-d)
        row_copy(d, along_sub(d), who, send_op, got_op, op_send, op_recv).wait()
        flip(who)
        return 0

    def send_ahead(step, chunk):
        halo(step, 0, chunk).start()
        halo(step, 1, chunk).start()
        if chunk == 0:
            y_halo(step, 0).start()

    def send_behind(step, chunk):
        def far_terms(l, _):
            terms = jnp.dot(flipped[table[1, l], 2 * BLK :], u[l], preferred_element_type=f32)
            zs[l] = terms[:BLK].astype(bf16)
            ts[l] = terms[BLK:].astype(bf16)
            return 0

        def y_terms(x, _):
            l = SITES - LX + x
            terms = jnp.dot(flipped[table[1, l], BLK : 2 * BLK], u[l], preferred_element_type=f32)
            ys[x] = terms.astype(bf16)
            return 0

        lax.fori_loop(LX * chunk, LX * chunk + LX, far_terms, 0, unroll=8)
        halo(step, 2, chunk).start()
        halo(step, 3, chunk).start()
        if chunk == LY - 1:
            lax.fori_loop(0, LX, y_terms, 0, unroll=8)
            y_halo(step, 1).start()

    def start_sums(step, stage):
        for d in range(1, 16):
            sum_copy(step, stage, d).start()

    def finish_sums(step, stage):
        buf = (rows, cols)[stage]
        others = buf.at[step, pl.ds(1, 15)]
        pltpu.make_async_remote_copy(
            src_ref=others, dst_ref=others, send_sem=sum_send.at[step, stage],
            recv_sem=sum_recv.at[step, stage], device_id={"sub": along_sub(1)}, device_id_type=MESH,
        ).wait()
        return jnp.sum(buf[step], axis=0)

    def send_rest(step):
        for chunk in range(1, LY):
            send_ahead(step, chunk)
            send_behind(step, chunk)

    def set_alpha(step, more):
        cols[step, 0] = finish_sums(step, 0)
        start_sums(step, 1)
        if more:
            send_rest(step + 1)
        both = finish_sums(step, 1)
        alpha[...] = both[0:1] / both[1:2]

    lax.fori_loop(0, SITES, begin, 0, unroll=4)
    alpha[...] = jnp.full_like(alpha, GUESS)
    for chunk in range(LY):
        send_ahead(0, chunk)
    lax.fori_loop(1, 16, take_blocks, 0)
    for chunk in range(LY):
        send_behind(0, chunk)

    def one_step(step, _):
        @pl.when(step > 0)
        def _():
            set_alpha(step - 1, True)

        def update(l, _):
            sol[l] = sol[l] + alpha[...] * v[l].astype(f32)
            new = res[l] - alpha[...] * image[l]
            res[l] = new
            v[l] = new.astype(bf16)
            return 0

        def behind(l, _):
            terms = jnp.dot(flipped[table[1, l], : 2 * BLK], v[l], preferred_element_type=f32)
            bx[l] = terms[:BLK]
            byl[l] = terms[BLK:]
            return 0

        lax.fori_loop(0, SITES, update, 0, unroll=8)
        lax.fori_loop(0, SITES, behind, 0, unroll=8)

        def near(chunk):
            def site(x, _):
                l = LX * chunk + x
                this = v[l]
                stack = [this, v[LX * chunk + lax.rem(x + 1, LX)]]
                if chunk < LY - 1:
                    stack.append(v[l + LX])
                total = jnp.dot(
                    got_op[table[1, l], :, : len(stack) * BLK], jnp.concatenate(stack, axis=0), preferred_element_type=f32
                )
                total = total + 4.0 * this.astype(f32) + bx[LX * chunk + lax.rem(x + LX - 1, LX)]
                if chunk > 0:
                    total = total + byl[l - LX]
                image[l] = total
                return 0

            lax.fori_loop(0, LX, site, 0, unroll=8)

        for chunk in range(LY):
            near(chunk)

        def far(chunk, carry):
            first = CUT // 2 if chunk == LY - 1 else CUT

            def site(x, carry):
                cross, power = carry
                l = LX * chunk + x
                stack = [uz[step, l], ut[step, l]]
                if chunk == LY - 1:
                    stack = [uy[step, x]] + stack
                stack = [jnp.zeros((WIDE - first - len(stack) * BLK, RHS), bf16)] + stack
                term = jnp.dot(
                    got_op[table[1, l], :, first:], jnp.concatenate(stack, axis=0), preferred_element_type=f32
                )
                term = term + bz[step, l].astype(f32) + bt[step, l].astype(f32)
                if chunk == 0:
                    term = term + by[step, x].astype(f32)
                held = halo_sum[l]
                outer = held + alpha[...] / GUESS * (term - held)
                halo_sum[l] = outer
                total = image[l] + outer
                image[l] = total
                old = res[l]
                u[l] = (old - GUESS * total).astype(bf16)
                cross = cross + jnp.sum((total * old).reshape(BLK // 8, 8, RHS), axis=0)
                power = power + jnp.sum((total * total).reshape(BLK // 8, 8, RHS), axis=0)
                return cross, power

            return lax.fori_loop(0, LX, site, carry, unroll=8)

        y_halo(step, 0).wait()
        y_halo(step, 1).wait()
        carry = (jnp.zeros((8, RHS), f32), jnp.zeros((8, RHS), f32))
        for chunk in range(LY):
            for kind in range(4):
                halo(step, kind, chunk).wait()
            carry = far(chunk, carry)
        rows[step, 0] = jnp.concatenate([jnp.sum(c, axis=0, keepdims=True) for c in carry], axis=0)
        start_sums(step, 0)

        @pl.when(step < STEPS - 1)
        def _():
            send_ahead(step + 1, 0)
            send_behind(step + 1, 0)

        return 0

    lax.fori_loop(0, STEPS, one_step, 0)
    set_alpha(STEPS - 1, False)

    def last(l, _):
        home[0, l] = (sol[l] + alpha[...] * v[l].astype(f32)).astype(bf16)
        home[1, l] = (res[l] - alpha[...] * image[l]).astype(bf16)
        return 0

    def home_copy(kind, chunk):
        part = pl.ds(LX * chunk, LX)
        return pltpu.make_async_remote_copy(
            src_ref=home.at[kind, part], dst_ref=(sol_out, res_out)[kind].at[part],
            send_sem=home_send.at[kind, chunk], recv_sem=home_recv.at[kind, chunk],
            device_id={"sub": here}, device_id_type=MESH,
        )

    for chunk in range(LY):
        lax.fori_loop(LX * chunk, LX * chunk + LX, last, 0, unroll=8)

        @pl.when(here != sub)
        def _():
            for kind in range(2):
                home_copy(kind, chunk).start()

    @pl.when(here == sub)
    def _():
        def keep(l, _):
            sol_out[l] = home[0, l]
            res_out[l] = home[1, l]
            return 0

        lax.fori_loop(0, SITES, keep, 0)

    @pl.when(here != sub)
    def _():
        for chunk in range(LY):
            for kind in range(2):
                home_copy(kind, chunk).wait()


def on_device(operator_fine, rhs_fine, fine_site):
    f32, bf16 = jnp.float32, jnp.bfloat16
    vector = (SITES, BLK, RHS)
    whole = pl.BlockSpec(memory_space=pltpu.VMEM)
    dma = pltpu.SemaphoreType.DMA
    sol, res = pl.pallas_call(
        kernel,
        out_shape=(jax.ShapeDtypeStruct(vector, bf16), jax.ShapeDtypeStruct(vector, bf16)),
        in_specs=[whole, pl.BlockSpec(memory_space=pl.ANY), pl.BlockSpec(memory_space=pl.ANY)],
        out_specs=(whole, whole),
        scratch_shapes=[
            pltpu.VMEM((SITES, BLK, WIDE), bf16),
            pltpu.VMEM(vector, bf16),
            pltpu.VMEM((2, 128), jnp.int32),
            pltpu.SMEM((2, 128), jnp.int32),
            pltpu.VMEM((SITES, BLK, WIDE), bf16),
            pltpu.VMEM(vector, bf16),
            pltpu.VMEM((SITES, BLK, WIDE), bf16),
            pltpu.VMEM(vector, bf16),
            pltpu.VMEM((SITES, 4 * BLK, BLK), bf16),
            pltpu.VMEM(vector, bf16),
            pltpu.VMEM((STEPS,) + vector, bf16),
            pltpu.VMEM((STEPS,) + vector, bf16),
            pltpu.VMEM((STEPS, LX, BLK, RHS), bf16),
            pltpu.VMEM(vector, bf16),
            pltpu.VMEM(vector, bf16),
            pltpu.VMEM((LX, BLK, RHS), bf16),
            pltpu.VMEM((STEPS,) + vector, bf16),
            pltpu.VMEM((STEPS,) + vector, bf16),
            pltpu.VMEM((STEPS, LX, BLK, RHS), bf16),
            pltpu.VMEM(vector, bf16),
            pltpu.VMEM(vector, f32),
            pltpu.VMEM(vector, f32),
            pltpu.VMEM(vector, f32),
            pltpu.VMEM(vector, f32),
            pltpu.VMEM(vector, f32),
            pltpu.VMEM(vector, f32),
            pltpu.VMEM((2,) + vector, bf16),
            pltpu.VMEM((1, RHS), f32),
            pltpu.VMEM((STEPS, 16, 2, RHS), f32),
            pltpu.VMEM((STEPS, 16, 2, RHS), f32),
            dma((16,)), dma((16,)), dma((16,)), dma((16,)),
            dma((STEPS, 4, LY)), dma((STEPS, 4, LY)),
            dma((STEPS, 2)), dma((STEPS, 2)),
            dma((STEPS, 2)), dma((STEPS, 2)), dma((2, LY)), dma((2, LY)), dma((3,)),
        ],
        compiler_params=pltpu.CompilerParams(
            collective_id=0, has_side_effects=True, vmem_limit_bytes=60 * 2**20
        ),
    )(fine_site.reshape(4, 128), operator_fine, rhs_fine)
    return sol.astype(f32), res.astype(f32)


def solution(mesh):
    in_specs = (P(("grp", "sub"), None, None), P(("grp", "sub"), None, None), P("grp"))
    out_specs = (P(("grp", "sub"), None, None), P(("grp", "sub"), None, None))
    return jax.shard_map(
        on_device, mesh=mesh, in_specs=in_specs, out_specs=out_specs, check_vma=False
    )
```

```python
import jax
import jax.numpy as jnp
from jax import lax
from jax.experimental import pallas as pl
from jax.experimental.pallas import tpu as pltpu
from jax.sharding import PartitionSpec as P

MESH = pl.DeviceIdType.MESH
STEPS = 4
LX = 8
LY = 4
SITES = 32
BLK = 96
RHS = 128
N_GRP = 16
N_SUB = 16
GUESS = 0.25
CUT = 256
WIDE = 5 * BLK


def place(logical):
    return logical % 2 * 8 + (8 - logical // 2) % 8


def logical_of(position):
    return (8 - position % 8) % 8 * 2 + position // 8


def tables(fine_site, sub):
    i32 = jnp.int32
    iota = lax.broadcasted_iota
    spread = jnp.concatenate([jnp.broadcast_to(fine_site[k : k + 1], (4, 128)) for k in range(4)], axis=0)
    device, lane = iota(i32, (N_SUB, 128), 0), iota(i32, (N_SUB, 128), 1)
    valid = lane // SITES == device % 4
    target = jnp.where(valid, place(spread // SITES % N_SUB), -1)
    mine = jnp.sum(jnp.where(device == sub, target + 1, 0), axis=0, keepdims=True) - 1
    down, across = iota(i32, (128, 128), 0), iota(i32, (128, 128), 1)
    column = jnp.sum(jnp.where(down == across, jnp.broadcast_to(mine, (128, 128)), 0), axis=1, keepdims=True)
    rank = jnp.sum(jnp.where((column == mine) & (across < down), 1, 0), axis=1, keepdims=True)
    slot = jnp.where(column >= 0, 2 * column + rank, -1)
    order = jnp.sum(jnp.where(slot == across, down % SITES, 0), axis=0, keepdims=True)
    hit = target == sub
    second = jnp.max(jnp.where(hit, lane, -1), axis=1, keepdims=True)
    site = spread % SITES
    site_b = jnp.sum(jnp.where(hit & (lane == second), site, 0), axis=1, keepdims=True)
    site_a = jnp.sum(jnp.where(hit & (lane < second), site, 0), axis=1, keepdims=True)
    inverse = jnp.sum(
        jnp.where(site_a == lane, 2 * device, 0) + jnp.where(site_b == lane, 2 * device + 1, 0), axis=0, keepdims=True
    )
    return jnp.minimum(jnp.concatenate([order, inverse], axis=0), SITES - 1)


def kernel(
    fine, op_hbm, rhs_hbm, sol_out, res_out,
    op, rhs, listed, table, send_op, dense, send_rhs, got_op, got_rhs, flipped,
    u, uz, ut, uy, zs, ts, ys, bz, bt, by, v, bx, byl, image, halo_sum, sol, res, home, stop,
    alpha, rows, cols,
    op_send, op_recv, rhs_send, rhs_recv, halo_send, halo_recv, y_send, y_recv, sum_send, sum_recv, home_send, home_recv, stop_send, stop_recv, local_sem,
):
    f32, bf16 = jnp.float32, jnp.bfloat16
    grp = lax.axis_index("grp")
    sub = lax.axis_index("sub")

    def along_sub(d):
        return lax.rem(sub + d + N_SUB, N_SUB)

    def along_grp(d):
        return lax.rem(grp + d + N_GRP, N_GRP)

    load_rhs = pltpu.make_async_copy(rhs_hbm, rhs, local_sem.at[0])
    load_op = pltpu.make_async_copy(op_hbm, op, local_sem.at[1])
    load_rhs.start()
    load_op.start()
    barrier = pltpu.get_barrier_semaphore()

    def greet(d, _):
        pl.semaphore_signal(barrier, inc=1, device_id={"sub": along_sub(d)}, device_id_type=MESH)
        pl.semaphore_signal(barrier, inc=1, device_id={"grp": along_grp(d)}, device_id_type=MESH)
        return 0

    lax.fori_loop(1, 16, greet, 0)

    def vector_copy(d, to, who):
        return pltpu.make_async_remote_copy(
            src_ref=send_rhs.at[pl.ds(2 * to, 2)], dst_ref=got_rhs.at[pl.ds(2 * who, 2)],
            send_sem=rhs_send.at[d], recv_sem=rhs_recv.at[d], device_id={"sub": to}, device_id_type=MESH,
        )

    def block_copy(d, to, who):
        return pltpu.make_async_remote_copy(
            src_ref=send_op.at[to], dst_ref=dense.at[who],
            send_sem=op_send.at[d], recv_sem=op_recv.at[d], device_id={"sub": to}, device_id_type=MESH,
        )

    listed[...] = tables(fine[...], sub)
    to_scalars = pltpu.make_async_copy(listed, table, local_sem.at[2])
    to_scalars.start()
    to_scalars.wait()
    load_rhs.wait()

    def pack_vectors(j, _):
        send_rhs[j] = rhs[table[0, j]]
        return 0

    lax.fori_loop(0, SITES, pack_vectors, 0, unroll=4)
    pl.semaphore_wait(barrier, 30)

    def send_vectors(d, _):
        to = along_sub(d)
        vector_copy(d, to, sub).start()
        return 0

    lax.fori_loop(1, 16, send_vectors, 0)
    load_op.wait()

    def send_blocks(d, _):
        to = along_sub(d)
        one, two = op[table[0, 2 * to]], op[table[0, 2 * to + 1]]
        for k, block in enumerate((one, two)):
            for tile in range(3):
                send_op[to, pl.ds((3 * k + tile) * BLK, BLK)] = block[:, 128 * tile : 128 * tile + 128]
        tail, rest = two[: BLK // 2, 384:], two[BLK // 2 :, 384:]
        side = jnp.concatenate([rest[:, :32], rest[:, 32:64], rest[:, 64:]], axis=0)
        main = jnp.concatenate([one[:, 384:], tail], axis=0)
        send_op[to, pl.ds(6 * BLK, 144)] = jnp.concatenate([main, side], axis=1)
        block_copy(d, to, sub).start()
        return 0

    lax.fori_loop(1, 16, send_blocks, 0)
    for k in range(2):
        got_rhs[2 * sub + k] = rhs[table[0, 2 * sub + k]]
        got_op[2 * sub + k] = op[table[0, 2 * sub + k]]

    sign_row = jnp.where(lax.broadcasted_iota(jnp.int32, (BLK, 1), 0) < BLK // 2, 1.0, -1.0).astype(f32)
    lane = lax.broadcasted_iota(jnp.int32, (1, WIDE), 1)
    sign_lane = jnp.where(lax.rem(lane, BLK) < BLK // 2, 1.0, -1.0).astype(f32)

    def flip(who):
        for k in range(2):
            signed = got_op[2 * who + k].astype(f32) * sign_row * sign_lane
            turned = jnp.transpose(signed)
            flipped[2 * who + k] = turned[BLK:].astype(bf16)

    flip(sub)

    def take_vectors(d, _):
        vector_copy(d, along_sub(d), along_sub(-d)).wait()
        return 0

    lax.fori_loop(1, 16, take_vectors, 0)

    here = logical_of(sub)
    half, layer = lax.rem(here, 2), here // 2
    other = place(2 * layer + 1 - half)
    z_down = place(2 * lax.rem(layer + 7, 8) + half)
    z_up = place(2 * lax.rem(layer + 1, 8) + half)
    t_down, t_up = along_grp(-1), along_grp(1)

    def halo(step, kind, chunk):
        part = pl.ds(LX * chunk, LX)
        src, dst, to = (
            (u.at[part], uz.at[step, part], {"sub": z_down}),
            (u.at[part], ut.at[step, part], {"grp": t_down}),
            (zs.at[part], bz.at[step, part], {"sub": z_up}),
            (ts.at[part], bt.at[step, part], {"grp": t_up}),
        )[kind]
        return pltpu.make_async_remote_copy(
            src_ref=src, dst_ref=dst, send_sem=halo_send.at[step, kind, chunk],
            recv_sem=halo_recv.at[step, kind, chunk], device_id=to, device_id_type=MESH,
        )

    def y_halo(step, kind):
        src, dst = (
            (u.at[pl.ds(0, LX)], uy.at[step]),
            (ys, by.at[step]),
        )[kind]
        return pltpu.make_async_remote_copy(
            src_ref=src, dst_ref=dst, send_sem=y_send.at[step, kind],
            recv_sem=y_recv.at[step, kind], device_id={"sub": other}, device_id_type=MESH,
        )

    def sum_copy(step, stage, d):
        to, buf = ({"sub": along_sub(d)}, rows) if stage == 0 else ({"grp": along_grp(d)}, cols)
        return pltpu.make_async_remote_copy(
            src_ref=buf.at[step, 0], dst_ref=buf.at[step, d], send_sem=sum_send.at[step, stage],
            recv_sem=sum_recv.at[step, stage], device_id=to, device_id_type=MESH,
        )

    def begin(l, _):
        start = got_rhs[table[1, l]]
        u[l] = start
        image[l] = start.astype(f32) * (-1.0 / GUESS)
        v[l] = jnp.zeros_like(start)
        res[l] = jnp.zeros((BLK, RHS), f32)
        sol[l] = jnp.zeros((BLK, RHS), f32)
        halo_sum[l] = jnp.zeros((BLK, RHS), f32)
        return 0

    def take_blocks(d, _):
        who = along_sub(-d)
        block_copy(d, along_sub(d), who).wait()
        for k in range(2):
            for tile in range(3):
                got_op[2 * who + k, :, 128 * tile : 128 * tile + 128] = dense[who, pl.ds((3 * k + tile) * BLK, BLK)]
        last_part = dense[who, pl.ds(6 * BLK, 144)]
        side = last_part[:, BLK:]
        rest = jnp.concatenate([side[:48], side[48:96], side[96:]], axis=1)
        got_op[2 * who, :, 384:] = last_part[:BLK, :BLK]
        got_op[2 * who + 1, :, 384:] = jnp.concatenate([last_part[BLK:, :BLK], rest], axis=0)
        flip(who)
        return 0

    def send_ahead(step, chunk):
        halo(step, 0, chunk).start()
        halo(step, 1, chunk).start()
        if chunk == 0:
            y_halo(step, 0).start()

    def send_behind(step, chunk):
        def far_terms(l, _):
            terms = jnp.dot(flipped[table[1, l], 2 * BLK :], u[l], preferred_element_type=f32)
            zs[l] = terms[:BLK].astype(bf16)
            ts[l] = terms[BLK:].astype(bf16)
            return 0

        def y_terms(x, _):
            l = SITES - LX + x
            terms = jnp.dot(flipped[table[1, l], BLK : 2 * BLK], u[l], preferred_element_type=f32)
            ys[x] = terms.astype(bf16)
            return 0

        lax.fori_loop(LX * chunk, LX * chunk + LX, far_terms, 0, unroll=8)
        halo(step, 2, chunk).start()
        halo(step, 3, chunk).start()
        if chunk == LY - 1:
            lax.fori_loop(0, LX, y_terms, 0, unroll=8)
            y_halo(step, 1).start()

    def start_sums(step, stage):
        for d in range(1, 16):
            sum_copy(step, stage, d).start()

    def finish_sums(step, stage):
        buf = (rows, cols)[stage]
        others = buf.at[step, pl.ds(1, 15)]
        pltpu.make_async_remote_copy(
            src_ref=others, dst_ref=others, send_sem=sum_send.at[step, stage],
            recv_sem=sum_recv.at[step, stage], device_id={"sub": along_sub(1)}, device_id_type=MESH,
        ).wait()
        return jnp.sum(buf[step], axis=0)

    def send_rest(step):
        for chunk in range(1, LY):
            send_ahead(step, chunk)
            send_behind(step, chunk)

    def set_alpha(step, more):
        cols[step, 0] = finish_sums(step, 0)
        start_sums(step, 1)
        if more:
            send_rest(step + 1)
        both = finish_sums(step, 1)
        alpha[...] = both[0:1] / both[1:2]

    lax.fori_loop(0, SITES, begin, 0, unroll=4)
    alpha[...] = jnp.full_like(alpha, GUESS)
    y_halo(0, 0).start()
    for chunk in range(LY):
        halo(0, 1, chunk).start()
    lax.fori_loop(1, 16, take_blocks, 0)
    for chunk in range(LY):
        halo(0, 0, chunk).start()
        send_behind(0, chunk)

    def one_step(step, _):
        @pl.when(step > 0)
        def _():
            set_alpha(step - 1, True)

        def update(l, _):
            sol[l] = sol[l] + alpha[...] * v[l].astype(f32)
            new = res[l] - alpha[...] * image[l]
            res[l] = new
            v[l] = new.astype(bf16)
            return 0

        def behind(l, _):
            terms = jnp.dot(flipped[table[1, l], : 2 * BLK], v[l], preferred_element_type=f32)
            bx[l] = terms[:BLK]
            byl[l] = terms[BLK:]
            return 0

        lax.fori_loop(0, SITES, update, 0, unroll=8)
        lax.fori_loop(0, SITES, behind, 0, unroll=8)

        def near(chunk):
            def site(x, _):
                l = LX * chunk + x
                this = v[l]
                stack = [this, v[LX * chunk + lax.rem(x + 1, LX)]]
                if chunk < LY - 1:
                    stack.append(v[l + LX])
                total = jnp.dot(
                    got_op[table[1, l], :, : len(stack) * BLK], jnp.concatenate(stack, axis=0), preferred_element_type=f32
                )
                total = total + 4.0 * this.astype(f32) + bx[LX * chunk + lax.rem(x + LX - 1, LX)]
                if chunk > 0:
                    total = total + byl[l - LX]
                image[l] = total
                return 0

            lax.fori_loop(0, LX, site, 0, unroll=8)

        for chunk in range(LY):
            near(chunk)

        def far(chunk, carry):
            first = CUT // 2 if chunk == LY - 1 else CUT

            def site(x, carry):
                cross, power = carry
                l = LX * chunk + x
                stack = [uz[step, l], ut[step, l]]
                if chunk == LY - 1:
                    stack = [uy[step, x]] + stack
                stack = [jnp.zeros((WIDE - first - len(stack) * BLK, RHS), bf16)] + stack
                term = jnp.dot(
                    got_op[table[1, l], :, first:], jnp.concatenate(stack, axis=0), preferred_element_type=f32
                )
                term = term + bz[step, l].astype(f32) + bt[step, l].astype(f32)
                if chunk == 0:
                    term = term + by[step, x].astype(f32)
                held = halo_sum[l]
                outer = held + alpha[...] / GUESS * (term - held)
                halo_sum[l] = outer
                total = image[l] + outer
                image[l] = total
                old = res[l]
                u[l] = (old - GUESS * total).astype(bf16)
                cross = cross + jnp.sum((total * old).reshape(BLK // 8, 8, RHS), axis=0)
                power = power + jnp.sum((total * total).reshape(BLK // 8, 8, RHS), axis=0)
                return cross, power

            return lax.fori_loop(0, LX, site, carry, unroll=8)

        y_halo(step, 0).wait()
        y_halo(step, 1).wait()
        carry = (jnp.zeros((8, RHS), f32), jnp.zeros((8, RHS), f32))
        for chunk in range(LY):
            for kind in range(4):
                halo(step, kind, chunk).wait()
            carry = far(chunk, carry)
        rows[step, 0] = jnp.concatenate([jnp.sum(c, axis=0, keepdims=True) for c in carry], axis=0)
        start_sums(step, 0)

        @pl.when(step < STEPS - 1)
        def _():
            send_ahead(step + 1, 0)
            send_behind(step + 1, 0)

        return 0

    lax.fori_loop(0, STEPS, one_step, 0)
    set_alpha(STEPS - 1, False)

    def last(l, _):
        home[0, l] = (sol[l] + alpha[...] * v[l].astype(f32)).astype(bf16)
        home[1, l] = (res[l] - alpha[...] * image[l]).astype(bf16)
        return 0

    column, height = sub // 8, sub % 8
    source_height = 4 + 3 * column
    far_owner = 8 - 5 * column
    outs = (sol_out, res_out)

    def beside(up):
        return 8 * column + lax.rem(source_height + (2 if up else 6), 8)

    is_source = height == source_height
    is_stop = [sub == beside(False), sub == beside(True)]

    def home_copy(kind, chunk):
        part = pl.ds(LX * chunk, LX)
        return pltpu.make_async_remote_copy(
            src_ref=home.at[kind, part], dst_ref=outs[kind].at[part],
            send_sem=home_send.at[kind, chunk], recv_sem=home_recv.at[kind, chunk],
            device_id={"sub": here}, device_id_type=MESH,
        )

    def first_leg(kind, chunk):
        return pltpu.make_async_remote_copy(
            src_ref=home.at[kind, pl.ds(LX * chunk, LX)], dst_ref=stop.at[kind, chunk // 2],
            send_sem=home_send.at[kind, chunk], recv_sem=stop_recv.at[kind, chunk // 2],
            device_id={"sub": beside(chunk % 2 == 1)}, device_id_type=MESH,
        )

    def second_leg(kind, chunk):
        return pltpu.make_async_remote_copy(
            src_ref=stop.at[kind, chunk // 2], dst_ref=outs[kind].at[pl.ds(LX * chunk, LX)],
            send_sem=stop_send.at[kind, chunk // 2], recv_sem=home_recv.at[kind, chunk],
            device_id={"sub": far_owner}, device_id_type=MESH,
        )

    for chunk in range(LY):
        lax.fori_loop(LX * chunk, LX * chunk + LX, last, 0, unroll=8)

        @pl.when(is_source)
        def _():
            for kind in range(2):
                first_leg(kind, chunk).start()

        @pl.when((here != sub) & (height != source_height))
        def _():
            for kind in range(2):
                home_copy(kind, chunk).start()

    for up in range(2):

        @pl.when(is_stop[up])
        def _():
            for chunk in (up, up + 2):
                for kind in range(2):
                    first_leg(kind, chunk).wait_recv()
                    second_leg(kind, chunk).start()

    @pl.when(here == sub)
    def _():
        def keep(l, _):
            sol_out[l] = home[0, l]
            res_out[l] = home[1, l]
            return 0

        lax.fori_loop(0, SITES, keep, 0)

    @pl.when(here != sub)
    def _():
        for chunk in range(LY):
            for kind in range(2):
                home_copy(kind, chunk).wait()

    for up in range(2):

        @pl.when(is_stop[up])
        def _():
            for chunk in (up, up + 2):
                for kind in range(2):
                    second_leg(kind, chunk).wait_send()


def on_device(operator_fine, rhs_fine, fine_site):
    f32, bf16 = jnp.float32, jnp.bfloat16
    vector = (SITES, BLK, RHS)
    whole = pl.BlockSpec(memory_space=pltpu.VMEM)
    dma = pltpu.SemaphoreType.DMA
    sol, res = pl.pallas_call(
        kernel,
        out_shape=(pltpu.VMEM(vector, bf16), pltpu.VMEM(vector, bf16)),
        in_specs=[whole, pl.BlockSpec(memory_space=pl.ANY), pl.BlockSpec(memory_space=pl.ANY)],
        out_specs=(whole, whole),
        scratch_shapes=[
            pltpu.VMEM((SITES, BLK, WIDE), bf16),
            pltpu.VMEM(vector, bf16),
            pltpu.VMEM((2, 128), jnp.int32),
            pltpu.SMEM((2, 128), jnp.int32),
            pltpu.VMEM((N_SUB, 720, 128), bf16),
            pltpu.VMEM((N_SUB, 720, 128), bf16),
            pltpu.VMEM(vector, bf16),
            pltpu.VMEM((SITES, BLK, WIDE), bf16),
            pltpu.VMEM(vector, bf16),
            pltpu.VMEM((SITES, 4 * BLK, BLK), bf16),
            pltpu.VMEM(vector, bf16),
            pltpu.VMEM((STEPS,) + vector, bf16),
            pltpu.VMEM((STEPS,) + vector, bf16),
            pltpu.VMEM((STEPS, LX, BLK, RHS), bf16),
            pltpu.VMEM(vector, bf16),
            pltpu.VMEM(vector, bf16),
            pltpu.VMEM((LX, BLK, RHS), bf16),
            pltpu.VMEM((STEPS,) + vector, bf16),
            pltpu.VMEM((STEPS,) + vector, bf16),
            pltpu.VMEM((STEPS, LX, BLK, RHS), bf16),
            pltpu.VMEM(vector, bf16),
            pltpu.VMEM(vector, f32),
            pltpu.VMEM(vector, f32),
            pltpu.VMEM(vector, f32),
            pltpu.VMEM(vector, f32),
            pltpu.VMEM(vector, f32),
            pltpu.VMEM(vector, f32),
            pltpu.VMEM((2,) + vector, bf16),
            pltpu.VMEM((2, 2, LX, BLK, RHS), bf16),
            pltpu.VMEM((1, RHS), f32),
            pltpu.VMEM((STEPS, 16, 2, RHS), f32),
            pltpu.VMEM((STEPS, 16, 2, RHS), f32),
            dma((16,)), dma((16,)), dma((16,)), dma((16,)),
            dma((STEPS, 4, LY)), dma((STEPS, 4, LY)),
            dma((STEPS, 2)), dma((STEPS, 2)),
            dma((STEPS, 2)), dma((STEPS, 2)), dma((2, LY)), dma((2, LY)), dma((2, 2)), dma((2, 2)), dma((3,)),
        ],
        compiler_params=pltpu.CompilerParams(
            collective_id=0, has_side_effects=True, vmem_limit_bytes=60 * 2**20
        ),
    )(fine_site.reshape(4, 128), operator_fine, rhs_fine)
    return sol.astype(f32), res.astype(f32)


def solution(mesh):
    in_specs = (P(("grp", "sub"), None, None), P(("grp", "sub"), None, None), P("grp"))
    out_specs = (P(("grp", "sub"), None, None), P(("grp", "sub"), None, None))
    return jax.shard_map(
        on_device, mesh=mesh, in_specs=in_specs, out_specs=out_specs, check_vma=False
    )
```

```python
import jax
import jax.numpy as jnp
from jax import lax
from jax.experimental import pallas as pl
from jax.experimental.pallas import tpu as pltpu
from jax.sharding import PartitionSpec as P

MESH = pl.DeviceIdType.MESH
STEPS = 4
LX = 8
LY = 4
SITES = 32
BLK = 96
RHS = 128
N_GRP = 16
N_SUB = 16
GUESS = 0.25
FIRST = 2
EARLY = 4
CUT = 256
WIDE = 5 * BLK


def place(logical):
    return logical % 2 * 8 + (8 - logical // 2) % 8


def logical_of(position):
    return (8 - position % 8) % 8 * 2 + position // 8


def tables(fine_site, sub):
    i32 = jnp.int32
    iota = lax.broadcasted_iota
    spread = jnp.concatenate([jnp.broadcast_to(fine_site[k : k + 1], (4, 128)) for k in range(4)], axis=0)
    device, lane = iota(i32, (N_SUB, 128), 0), iota(i32, (N_SUB, 128), 1)
    valid = lane // SITES == device % 4
    target = jnp.where(valid, place(spread // SITES % N_SUB), -1)
    mine = jnp.sum(jnp.where(device == sub, target + 1, 0), axis=0, keepdims=True) - 1
    down, across = iota(i32, (128, 128), 0), iota(i32, (128, 128), 1)
    column = jnp.sum(jnp.where(down == across, jnp.broadcast_to(mine, (128, 128)), 0), axis=1, keepdims=True)
    rank = jnp.sum(jnp.where((column == mine) & (across < down), 1, 0), axis=1, keepdims=True)
    slot = jnp.where(column >= 0, 2 * column + rank, -1)
    order = jnp.sum(jnp.where(slot == across, down % SITES, 0), axis=0, keepdims=True)
    hit = target == sub
    second = jnp.max(jnp.where(hit, lane, -1), axis=1, keepdims=True)
    site = spread % SITES
    site_b = jnp.sum(jnp.where(hit & (lane == second), site, 0), axis=1, keepdims=True)
    site_a = jnp.sum(jnp.where(hit & (lane < second), site, 0), axis=1, keepdims=True)
    inverse = jnp.sum(
        jnp.where(site_a == lane, 2 * device, 0) + jnp.where(site_b == lane, 2 * device + 1, 0), axis=0, keepdims=True
    )
    return jnp.minimum(jnp.concatenate([order, inverse], axis=0), SITES - 1)


def kernel(
    fine, op_hbm, rhs_hbm, sol_out, res_out,
    op, rhs, listed, table, send_op, dense, send_rhs, got_op, got_rhs, flipped,
    u, uz, ut, uy, zs, ts, ys, bz, bt, by, v, bx, byl, image, halo_sum, sol, res, home, stop, early,
    alpha, rows, cols,
    op_send, op_recv, rhs_send, rhs_recv, halo_send, halo_recv, y_send, y_recv, sum_send, sum_recv, home_send, home_recv, stop_send, stop_recv,
    early_send, early_recv, local_sem,
):
    f32, bf16 = jnp.float32, jnp.bfloat16
    grp = lax.axis_index("grp")
    sub = lax.axis_index("sub")

    def along_sub(d):
        return lax.rem(sub + d + N_SUB, N_SUB)

    def spread_out(turn):
        return lax.rem(5 * turn, N_SUB)

    def along_grp(d):
        return lax.rem(grp + d + N_GRP, N_GRP)

    def partner(stage, d):
        if stage == 0:
            return {"grp": grp // 2 * 2 + lax.rem(grp + d // 8, 2), "sub": sub // 8 * 8 + lax.rem(sub + d, 8)}
        return {"grp": lax.rem(grp + d // 2 * 2, N_GRP), "sub": lax.rem(sub + d % 2 * 8, N_SUB)}

    load_rhs = pltpu.make_async_copy(rhs_hbm, rhs, local_sem.at[0])
    load_op = pltpu.make_async_copy(op_hbm, op, local_sem.at[1])
    load_rhs.start()
    load_op.start()
    barrier = pltpu.get_barrier_semaphore()

    def greet(d, _):
        pl.semaphore_signal(barrier, inc=1, device_id={"sub": along_sub(d)}, device_id_type=MESH)
        return 0

    lax.fori_loop(1, 16, greet, 0)
    for d in range(8, 16):
        pl.semaphore_signal(barrier, inc=1, device_id=partner(0, d), device_id_type=MESH)
    for d in range(2, 16):
        pl.semaphore_signal(barrier, inc=1, device_id=partner(1, d), device_id_type=MESH)
    across = lax.rem(grp + jnp.where(grp % 2 == 0, N_GRP - 1, 1), N_GRP)
    pl.semaphore_signal(barrier, inc=1, device_id={"grp": across}, device_id_type=MESH)

    def vector_copy(d, to, who):
        return pltpu.make_async_remote_copy(
            src_ref=send_rhs.at[pl.ds(2 * to, 2)], dst_ref=got_rhs.at[pl.ds(2 * who, 2)],
            send_sem=rhs_send.at[d], recv_sem=rhs_recv.at[d], device_id={"sub": to}, device_id_type=MESH,
        )

    def block_copy(d, to, who):
        return pltpu.make_async_remote_copy(
            src_ref=send_op.at[to], dst_ref=dense.at[who],
            send_sem=op_send.at[d], recv_sem=op_recv.at[d], device_id={"sub": to}, device_id_type=MESH,
        )

    listed[...] = tables(fine[...], sub)
    to_scalars = pltpu.make_async_copy(listed, table, local_sem.at[2])
    to_scalars.start()
    to_scalars.wait()
    load_rhs.wait()

    def pack_vectors(j, _):
        send_rhs[j] = rhs[table[0, j]]
        return 0

    lax.fori_loop(0, SITES, pack_vectors, 0, unroll=4)
    pl.semaphore_wait(barrier, 15 + 8 + 14 + 1)

    def send_vectors(turn, _):
        d = spread_out(turn)
        to = along_sub(d)
        vector_copy(d, to, sub).start()
        return 0

    lax.fori_loop(1, 16, send_vectors, 0)
    load_op.wait()

    def send_blocks(turn, _):
        d = spread_out(turn)
        to = along_sub(d)
        one, two = op[table[0, 2 * to]], op[table[0, 2 * to + 1]]
        for k, block in enumerate((one, two)):
            for tile in range(3):
                send_op[to, pl.ds((3 * k + tile) * BLK, BLK)] = block[:, 128 * tile : 128 * tile + 128]
        tail, rest = two[: BLK // 2, 384:], two[BLK // 2 :, 384:]
        side = jnp.concatenate([rest[:, :32], rest[:, 32:64], rest[:, 64:]], axis=0)
        main = jnp.concatenate([one[:, 384:], tail], axis=0)
        send_op[to, pl.ds(6 * BLK, 144)] = jnp.concatenate([main, side], axis=1)
        block_copy(d, to, sub).start()
        return 0

    lax.fori_loop(1, 16, send_blocks, 0)
    for k in range(2):
        got_rhs[2 * sub + k] = rhs[table[0, 2 * sub + k]]
        got_op[2 * sub + k] = op[table[0, 2 * sub + k]]

    sign_row = jnp.where(lax.broadcasted_iota(jnp.int32, (BLK, 1), 0) < BLK // 2, 1.0, -1.0).astype(f32)
    lane = lax.broadcasted_iota(jnp.int32, (1, WIDE), 1)
    sign_lane = jnp.where(lax.rem(lane, BLK) < BLK // 2, 1.0, -1.0).astype(f32)

    def flip(who):
        for k in range(2):
            signed = got_op[2 * who + k].astype(f32) * sign_row * sign_lane
            turned = jnp.transpose(signed)
            flipped[2 * who + k] = turned[BLK:].astype(bf16)

    flip(sub)

    def take_vectors(turn, _):
        d = spread_out(turn)
        vector_copy(d, along_sub(d), along_sub(-d)).wait()
        return 0

    lax.fori_loop(1, 16, take_vectors, 0)

    here = logical_of(sub)
    half, layer = lax.rem(here, 2), here // 2
    other = place(2 * layer + 1 - half)
    z_down = place(2 * lax.rem(layer + 7, 8) + half)
    z_up = place(2 * lax.rem(layer + 1, 8) + half)
    t_down, t_up = along_grp(-1), along_grp(1)

    def halo(step, kind, chunk):
        part = pl.ds(LX * chunk, LX)
        src, dst, to = (
            (u.at[part], uz.at[step, part], {"sub": z_down}),
            (u.at[part], ut.at[step, part], {"grp": t_down}),
            (zs.at[part], bz.at[step, part], {"sub": z_up}),
            (ts.at[part], bt.at[step, part], {"grp": t_up}),
        )[kind]
        return pltpu.make_async_remote_copy(
            src_ref=src, dst_ref=dst, send_sem=halo_send.at[step, kind, chunk],
            recv_sem=halo_recv.at[step, kind, chunk], device_id=to, device_id_type=MESH,
        )

    def y_halo(step, kind):
        src, dst = (
            (u.at[pl.ds(0, LX)], uy.at[step]),
            (ys, by.at[step]),
        )[kind]
        return pltpu.make_async_remote_copy(
            src_ref=src, dst_ref=dst, send_sem=y_send.at[step, kind],
            recv_sem=y_recv.at[step, kind], device_id={"sub": other}, device_id_type=MESH,
        )

    def sum_copy(step, stage, d):
        to, buf = partner(stage, d), (rows, cols)[stage]
        return pltpu.make_async_remote_copy(
            src_ref=buf.at[step, 0], dst_ref=buf.at[step, d], send_sem=sum_send.at[step, stage],
            recv_sem=sum_recv.at[step, stage], device_id=to, device_id_type=MESH,
        )

    def begin(l, _):
        start = got_rhs[table[1, l]]
        u[l] = start
        image[l] = start.astype(f32) * (-1.0 / GUESS)
        v[l] = jnp.zeros_like(start)
        res[l] = jnp.zeros((BLK, RHS), f32)
        sol[l] = jnp.zeros((BLK, RHS), f32)
        halo_sum[l] = jnp.zeros((BLK, RHS), f32)
        return 0

    def take_blocks(turn, _):
        d = spread_out(turn)
        who = along_sub(-d)
        block_copy(d, along_sub(d), who).wait()
        for k in range(2):
            for tile in range(3):
                got_op[2 * who + k, :, 128 * tile : 128 * tile + 128] = dense[who, pl.ds((3 * k + tile) * BLK, BLK)]
        last_part = dense[who, pl.ds(6 * BLK, 144)]
        side = last_part[:, BLK:]
        rest = jnp.concatenate([side[:48], side[48:96], side[96:]], axis=1)
        got_op[2 * who, :, 384:] = last_part[:BLK, :BLK]
        got_op[2 * who + 1, :, 384:] = jnp.concatenate([last_part[BLK:, :BLK], rest], axis=0)
        flip(who)
        return 0

    def send_ahead(step, chunk):
        halo(step, 0, chunk).start()
        halo(step, 1, chunk).start()
        if chunk == 0:
            y_halo(step, 0).start()

    def send_behind(step, chunk):
        def far_terms(l, _):
            terms = jnp.dot(flipped[table[1, l], 2 * BLK :], u[l], preferred_element_type=f32)
            zs[l] = terms[:BLK].astype(bf16)
            ts[l] = terms[BLK:].astype(bf16)
            return 0

        def y_terms(x, _):
            l = SITES - LX + x
            terms = jnp.dot(flipped[table[1, l], BLK : 2 * BLK], u[l], preferred_element_type=f32)
            ys[x] = terms.astype(bf16)
            return 0

        lax.fori_loop(LX * chunk, LX * chunk + LX, far_terms, 0, unroll=8)
        halo(step, 2, chunk).start()
        halo(step, 3, chunk).start()
        if chunk == LY - 1:
            lax.fori_loop(0, LX, y_terms, 0, unroll=8)
            y_halo(step, 1).start()

    def start_sums(step, stage):
        for d in range(1, 16):
            sum_copy(step, stage, d).start()

    def finish_sums(step, stage):
        buf = (rows, cols)[stage]
        others = buf.at[step, pl.ds(1, 15)]
        pltpu.make_async_remote_copy(
            src_ref=others, dst_ref=others, send_sem=sum_send.at[step, stage],
            recv_sem=sum_recv.at[step, stage], device_id={"sub": along_sub(1)}, device_id_type=MESH,
        ).wait()
        return jnp.sum(buf[step], axis=0)

    def send_rest(step):
        for chunk in range(FIRST, LY):
            send_ahead(step, chunk)
            send_behind(step, chunk)

    def early_copy(kind):
        part = pl.ds(0, EARLY)
        return pltpu.make_async_remote_copy(
            src_ref=(home.at[0, part], v.at[part], u.at[part])[kind], dst_ref=early.at[kind],
            send_sem=early_send.at[kind], recv_sem=early_recv.at[kind],
            device_id={"sub": here}, device_id_type=MESH,
        )

    def set_alpha(step, more):
        cols[step, 0] = finish_sums(step, 0)
        start_sums(step, 1)
        if more:
            send_rest(step + 1)
        else:

            @pl.when(here != sub)
            def _():
                early_copy(2).start()

        both = finish_sums(step, 1)
        alpha[...] = both[0:1] / both[1:2]

    lax.fori_loop(0, SITES, begin, 0, unroll=4)
    alpha[...] = jnp.full_like(alpha, GUESS)
    y_halo(0, 0).start()
    for chunk in range(LY):
        halo(0, 1, chunk).start()
    lax.fori_loop(1, 16, take_blocks, 0)
    for chunk in range(LY):
        halo(0, 0, chunk).start()
        send_behind(0, chunk)

    def one_step(step, _):
        @pl.when(step > 0)
        def _():
            set_alpha(step - 1, True)

        def update(l, _):
            sol[l] = sol[l] + alpha[...] * v[l].astype(f32)
            new = res[l] - alpha[...] * image[l]
            res[l] = new
            v[l] = new.astype(bf16)
            return 0

        def behind(l, _):
            terms = jnp.dot(flipped[table[1, l], : 2 * BLK], v[l], preferred_element_type=f32)
            bx[l] = terms[:BLK]
            byl[l] = terms[BLK:]
            return 0

        lax.fori_loop(0, SITES, update, 0, unroll=8)
        lax.fori_loop(0, SITES, behind, 0, unroll=8)

        def near(chunk):
            def site(x, _):
                l = LX * chunk + x
                this = v[l]
                stack = [this, v[LX * chunk + lax.rem(x + 1, LX)]]
                if chunk < LY - 1:
                    stack.append(v[l + LX])
                total = jnp.dot(
                    got_op[table[1, l], :, : len(stack) * BLK], jnp.concatenate(stack, axis=0), preferred_element_type=f32
                )
                total = total + 4.0 * this.astype(f32) + bx[LX * chunk + lax.rem(x + LX - 1, LX)]
                if chunk > 0:
                    total = total + byl[l - LX]
                image[l] = total
                return 0

            lax.fori_loop(0, LX, site, 0, unroll=8)

        for chunk in range(LY):
            near(chunk)

        def far(chunk, carry):
            first = CUT // 2 if chunk == LY - 1 else CUT

            def site(x, carry):
                cross, power = carry
                l = LX * chunk + x
                stack = [uz[step, l], ut[step, l]]
                if chunk == LY - 1:
                    stack = [uy[step, x]] + stack
                stack = [jnp.zeros((WIDE - first - len(stack) * BLK, RHS), bf16)] + stack
                term = jnp.dot(
                    got_op[table[1, l], :, first:], jnp.concatenate(stack, axis=0), preferred_element_type=f32
                )
                term = term + bz[step, l].astype(f32) + bt[step, l].astype(f32)
                if chunk == 0:
                    term = term + by[step, x].astype(f32)
                held = halo_sum[l]
                outer = held + alpha[...] / GUESS * (term - held)
                halo_sum[l] = outer
                total = image[l] + outer
                image[l] = total
                old = res[l]
                u[l] = (old - GUESS * total).astype(bf16)
                cross = cross + jnp.sum((total * old).reshape(BLK // 8, 8, RHS), axis=0)
                power = power + jnp.sum((total * total).reshape(BLK // 8, 8, RHS), axis=0)
                return cross, power

            return lax.fori_loop(0, LX, site, carry, unroll=8)

        y_halo(step, 0).wait()
        y_halo(step, 1).wait()
        carry = (jnp.zeros((8, RHS), f32), jnp.zeros((8, RHS), f32))
        for chunk in range(LY):
            for kind in range(4):
                halo(step, kind, chunk).wait()
            carry = far(chunk, carry)
        rows[step, 0] = jnp.concatenate([jnp.sum(c, axis=0, keepdims=True) for c in carry], axis=0)
        start_sums(step, 0)

        @pl.when(step < STEPS - 1)
        def _():
            for chunk in range(FIRST):
                send_ahead(step + 1, chunk)
                send_behind(step + 1, chunk)

        @pl.when((step == STEPS - 1) & (here != sub))
        def _():
            for l in range(EARLY):
                home[0, l] = sol[l].astype(bf16)
            early_copy(0).start()
            early_copy(1).start()

        return 0

    lax.fori_loop(0, STEPS, one_step, 0)
    set_alpha(STEPS - 1, False)

    def last(l, _):
        home[0, l] = (sol[l] + alpha[...] * v[l].astype(f32)).astype(bf16)
        home[1, l] = (res[l] - alpha[...] * image[l]).astype(bf16)
        return 0

    column, height = sub // 8, sub % 8
    source_height = 4 + 3 * column
    far_owner = 8 - 5 * column
    outs = (sol_out, res_out)

    def beside(up):
        return 8 * column + lax.rem(source_height + (2 if up else 6), 8)

    is_source = height == source_height
    is_stop = [sub == beside(False), sub == beside(True)]

    def span(chunk):
        return (EARLY, LX - EARLY) if chunk == 0 else (LX * chunk, LX)

    def home_copy(kind, chunk):
        part = pl.ds(*span(chunk))
        return pltpu.make_async_remote_copy(
            src_ref=home.at[kind, part], dst_ref=outs[kind].at[part],
            send_sem=home_send.at[kind, chunk], recv_sem=home_recv.at[kind, chunk],
            device_id={"sub": here}, device_id_type=MESH,
        )

    def first_leg(kind, chunk):
        return pltpu.make_async_remote_copy(
            src_ref=home.at[kind, pl.ds(*span(chunk))], dst_ref=stop.at[kind, chunk // 2, pl.ds(0, span(chunk)[1])],
            send_sem=home_send.at[kind, chunk], recv_sem=stop_recv.at[kind, chunk // 2],
            device_id={"sub": beside(chunk % 2 == 1)}, device_id_type=MESH,
        )

    def second_leg(kind, chunk):
        return pltpu.make_async_remote_copy(
            src_ref=stop.at[kind, chunk // 2, pl.ds(0, span(chunk)[1])], dst_ref=outs[kind].at[pl.ds(*span(chunk))],
            send_sem=stop_send.at[kind, chunk // 2], recv_sem=home_recv.at[kind, chunk],
            device_id={"sub": far_owner}, device_id_type=MESH,
        )

    for chunk in range(LY):
        lax.fori_loop(span(chunk)[0], sum(span(chunk)), last, 0, unroll=4)

        @pl.when(is_source)
        def _():
            for kind in range(2):
                first_leg(kind, chunk).start()

        @pl.when((here != sub) & (height != source_height))
        def _():
            for kind in range(2):
                home_copy(kind, chunk).start()

    for up in range(2):

        @pl.when(is_stop[up])
        def _():
            for chunk in (up, up + 2):
                for kind in range(2):
                    first_leg(kind, chunk).wait_recv()
                    second_leg(kind, chunk).start()

    @pl.when(here == sub)
    def _():
        lax.fori_loop(0, EARLY, last, 0, unroll=4)

        def keep(l, _):
            sol_out[l] = home[0, l]
            res_out[l] = home[1, l]
            return 0

        lax.fori_loop(0, SITES, keep, 0)

    @pl.when(here != sub)
    def _():
        for kind in range(3):
            early_copy(kind).wait()
        for l in range(EARLY):
            old = early[1, l].astype(f32)
            sol_out[l] = (early[0, l].astype(f32) + alpha[...] * old).astype(bf16)
            res_out[l] = (old + alpha[...] / GUESS * (early[2, l].astype(f32) - old)).astype(bf16)
        for chunk in range(LY):
            for kind in range(2):
                home_copy(kind, chunk).wait()

    for up in range(2):

        @pl.when(is_stop[up])
        def _():
            for chunk in (up, up + 2):
                for kind in range(2):
                    second_leg(kind, chunk).wait_send()


def on_device(operator_fine, rhs_fine, fine_site):
    f32, bf16 = jnp.float32, jnp.bfloat16
    vector = (SITES, BLK, RHS)
    whole = pl.BlockSpec(memory_space=pltpu.VMEM)
    dma = pltpu.SemaphoreType.DMA
    sol, res = pl.pallas_call(
        kernel,
        out_shape=(pltpu.VMEM(vector, bf16), pltpu.VMEM(vector, bf16)),
        in_specs=[whole, pl.BlockSpec(memory_space=pl.ANY), pl.BlockSpec(memory_space=pl.ANY)],
        out_specs=(whole, whole),
        scratch_shapes=[
            pltpu.VMEM((SITES, BLK, WIDE), bf16),
            pltpu.VMEM(vector, bf16),
            pltpu.VMEM((2, 128), jnp.int32),
            pltpu.SMEM((2, 128), jnp.int32),
            pltpu.VMEM((N_SUB, 720, 128), bf16),
            pltpu.VMEM((N_SUB, 720, 128), bf16),
            pltpu.VMEM(vector, bf16),
            pltpu.VMEM((SITES, BLK, WIDE), bf16),
            pltpu.VMEM(vector, bf16),
            pltpu.VMEM((SITES, 4 * BLK, BLK), bf16),
            pltpu.VMEM(vector, bf16),
            pltpu.VMEM((STEPS,) + vector, bf16),
            pltpu.VMEM((STEPS,) + vector, bf16),
            pltpu.VMEM((STEPS, LX, BLK, RHS), bf16),
            pltpu.VMEM(vector, bf16),
            pltpu.VMEM(vector, bf16),
            pltpu.VMEM((LX, BLK, RHS), bf16),
            pltpu.VMEM((STEPS,) + vector, bf16),
            pltpu.VMEM((STEPS,) + vector, bf16),
            pltpu.VMEM((STEPS, LX, BLK, RHS), bf16),
            pltpu.VMEM(vector, bf16),
            pltpu.VMEM(vector, f32),
            pltpu.VMEM(vector, f32),
            pltpu.VMEM(vector, f32),
            pltpu.VMEM(vector, f32),
            pltpu.VMEM(vector, f32),
            pltpu.VMEM(vector, f32),
            pltpu.VMEM((2,) + vector, bf16),
            pltpu.VMEM((2, 2, LX, BLK, RHS), bf16),
            pltpu.VMEM((3, EARLY, BLK, RHS), bf16),
            pltpu.VMEM((1, RHS), f32),
            pltpu.VMEM((STEPS, 16, 2, RHS), f32),
            pltpu.VMEM((STEPS, 16, 2, RHS), f32),
            dma((16,)), dma((16,)), dma((16,)), dma((16,)),
            dma((STEPS, 4, LY)), dma((STEPS, 4, LY)),
            dma((STEPS, 2)), dma((STEPS, 2)),
            dma((STEPS, 2)), dma((STEPS, 2)), dma((2, LY)), dma((2, LY)), dma((2, 2)), dma((2, 2)),
            dma((3,)), dma((3,)), dma((3,)),
        ],
        compiler_params=pltpu.CompilerParams(
            collective_id=0, has_side_effects=True, vmem_limit_bytes=60 * 2**20
        ),
    )(fine_site.reshape(4, 128), operator_fine, rhs_fine)
    return sol.astype(f32), res.astype(f32)


def solution(mesh):
    in_specs = (P(("grp", "sub"), None, None), P(("grp", "sub"), None, None), P("grp"))
    out_specs = (P(("grp", "sub"), None, None), P(("grp", "sub"), None, None))
    return jax.shard_map(
        on_device, mesh=mesh, in_specs=in_specs, out_specs=out_specs, check_vma=False
    )
```

```python
import jax
import jax.numpy as jnp
from jax import lax
from jax.experimental import pallas as pl
from jax.experimental.pallas import tpu as pltpu
from jax.sharding import PartitionSpec as P

MESH = pl.DeviceIdType.MESH
STEPS = 4
LX = 8
LY = 4
SITES = 32
BLK = 96
RHS = 128
N_GRP = 16
N_SUB = 16
GUESS = 0.25
FIRST = 2
EARLY = 6
CUT = 256
WIDE = 5 * BLK


def place(logical):
    return logical % 2 * 8 + (8 - logical // 2) % 8


def logical_of(position):
    return (8 - position % 8) % 8 * 2 + position // 8


def tables(fine_site, sub):
    i32 = jnp.int32
    iota = lax.broadcasted_iota
    spread = jnp.concatenate([jnp.broadcast_to(fine_site[k : k + 1], (4, 128)) for k in range(4)], axis=0)
    device, lane = iota(i32, (N_SUB, 128), 0), iota(i32, (N_SUB, 128), 1)
    valid = lane // SITES == device % 4
    target = jnp.where(valid, place(spread // SITES % N_SUB), -1)
    mine = jnp.sum(jnp.where(device == sub, target + 1, 0), axis=0, keepdims=True) - 1
    down, across = iota(i32, (128, 128), 0), iota(i32, (128, 128), 1)
    column = jnp.sum(jnp.where(down == across, jnp.broadcast_to(mine, (128, 128)), 0), axis=1, keepdims=True)
    rank = jnp.sum(jnp.where((column == mine) & (across < down), 1, 0), axis=1, keepdims=True)
    slot = jnp.where(column >= 0, 2 * column + rank, -1)
    order = jnp.sum(jnp.where(slot == across, down % SITES, 0), axis=0, keepdims=True)
    hit = target == sub
    second = jnp.max(jnp.where(hit, lane, -1), axis=1, keepdims=True)
    site = spread % SITES
    site_b = jnp.sum(jnp.where(hit & (lane == second), site, 0), axis=1, keepdims=True)
    site_a = jnp.sum(jnp.where(hit & (lane < second), site, 0), axis=1, keepdims=True)
    inverse = jnp.sum(
        jnp.where(site_a == lane, 2 * device, 0) + jnp.where(site_b == lane, 2 * device + 1, 0), axis=0, keepdims=True
    )
    return jnp.minimum(jnp.concatenate([order, inverse], axis=0), SITES - 1)


def kernel(
    fine, op_hbm, rhs_hbm, sol_out, res_out,
    op, rhs, listed, table, send_op, dense, send_rhs, got_op, got_rhs, flipped,
    u, uz, ut, uy, zs, ts, ys, bz, bt, by, v, bx, byl, image, halo_sum, sol, res, home, stop, early,
    alpha, rows, cols,
    op_send, op_recv, rhs_send, rhs_recv, halo_send, halo_recv, y_send, y_recv, sum_send, sum_recv, home_send, home_recv, stop_send, stop_recv,
    early_send, early_recv, local_sem,
):
    f32, bf16 = jnp.float32, jnp.bfloat16
    grp = lax.axis_index("grp")
    sub = lax.axis_index("sub")

    def along_sub(d):
        return lax.rem(sub + d + N_SUB, N_SUB)

    def spread_out(turn):
        return lax.rem(5 * turn, N_SUB)

    def along_grp(d):
        return lax.rem(grp + d + N_GRP, N_GRP)

    def partner(stage, d):
        if stage == 0:
            return {"grp": grp // 2 * 2 + lax.rem(grp + d // 8, 2), "sub": sub // 8 * 8 + lax.rem(sub + d, 8)}
        return {"grp": lax.rem(grp + d // 2 * 2, N_GRP), "sub": lax.rem(sub + d % 2 * 8, N_SUB)}

    load_rhs = pltpu.make_async_copy(rhs_hbm, rhs, local_sem.at[0])
    load_op = pltpu.make_async_copy(op_hbm, op, local_sem.at[1])
    load_rhs.start()
    load_op.start()
    barrier = pltpu.get_barrier_semaphore()

    def greet(d, _):
        pl.semaphore_signal(barrier, inc=1, device_id={"sub": along_sub(d)}, device_id_type=MESH)
        return 0

    lax.fori_loop(1, 16, greet, 0)
    for d in range(8, 16):
        pl.semaphore_signal(barrier, inc=1, device_id=partner(0, d), device_id_type=MESH)
    for d in range(2, 16):
        pl.semaphore_signal(barrier, inc=1, device_id=partner(1, d), device_id_type=MESH)
    across = lax.rem(grp + jnp.where(grp % 2 == 0, N_GRP - 1, 1), N_GRP)
    pl.semaphore_signal(barrier, inc=1, device_id={"grp": across}, device_id_type=MESH)

    def vector_copy(d, to, who):
        return pltpu.make_async_remote_copy(
            src_ref=send_rhs.at[pl.ds(2 * to, 2)], dst_ref=got_rhs.at[pl.ds(2 * who, 2)],
            send_sem=rhs_send.at[d], recv_sem=rhs_recv.at[d], device_id={"sub": to}, device_id_type=MESH,
        )

    def block_copy(d, to, who):
        return pltpu.make_async_remote_copy(
            src_ref=send_op.at[to], dst_ref=dense.at[who],
            send_sem=op_send.at[d], recv_sem=op_recv.at[d], device_id={"sub": to}, device_id_type=MESH,
        )

    listed[...] = tables(fine[...], sub)
    to_scalars = pltpu.make_async_copy(listed, table, local_sem.at[2])
    to_scalars.start()
    to_scalars.wait()
    load_rhs.wait()

    def pack_vectors(j, _):
        send_rhs[j] = rhs[table[0, j]]
        return 0

    lax.fori_loop(0, SITES, pack_vectors, 0, unroll=4)
    pl.semaphore_wait(barrier, 15 + 8 + 14 + 1)

    def send_vectors(turn, _):
        d = spread_out(turn)
        to = along_sub(d)
        vector_copy(d, to, sub).start()
        return 0

    lax.fori_loop(1, 16, send_vectors, 0)
    load_op.wait()

    def send_blocks(turn, _):
        d = spread_out(turn)
        to = along_sub(d)
        one, two = op[table[0, 2 * to]], op[table[0, 2 * to + 1]]
        for k, block in enumerate((one, two)):
            for tile in range(3):
                send_op[to, pl.ds((3 * k + tile) * BLK, BLK)] = block[:, 128 * tile : 128 * tile + 128]
        tail, rest = two[: BLK // 2, 384:], two[BLK // 2 :, 384:]
        side = jnp.concatenate([rest[:, :32], rest[:, 32:64], rest[:, 64:]], axis=0)
        main = jnp.concatenate([one[:, 384:], tail], axis=0)
        send_op[to, pl.ds(6 * BLK, 144)] = jnp.concatenate([main, side], axis=1)
        block_copy(d, to, sub).start()
        return 0

    lax.fori_loop(1, 16, send_blocks, 0)
    for k in range(2):
        got_rhs[2 * sub + k] = rhs[table[0, 2 * sub + k]]
        got_op[2 * sub + k] = op[table[0, 2 * sub + k]]

    sign_row = jnp.where(lax.broadcasted_iota(jnp.int32, (BLK, 1), 0) < BLK // 2, 1.0, -1.0).astype(f32)
    lane = lax.broadcasted_iota(jnp.int32, (1, WIDE), 1)
    sign_lane = jnp.where(lax.rem(lane, BLK) < BLK // 2, 1.0, -1.0).astype(f32)

    def flip(who):
        for k in range(2):
            signed = got_op[2 * who + k].astype(f32) * sign_row * sign_lane
            turned = jnp.transpose(signed)
            flipped[2 * who + k] = turned[BLK:].astype(bf16)

    flip(sub)

    def take_vectors(turn, _):
        d = spread_out(turn)
        vector_copy(d, along_sub(d), along_sub(-d)).wait()
        return 0

    lax.fori_loop(1, 16, take_vectors, 0)

    here = logical_of(sub)
    half, layer = lax.rem(here, 2), here // 2
    other = place(2 * layer + 1 - half)
    z_down = place(2 * lax.rem(layer + 7, 8) + half)
    z_up = place(2 * lax.rem(layer + 1, 8) + half)
    t_down, t_up = along_grp(-1), along_grp(1)

    def halo(step, kind, chunk):
        part = pl.ds(LX * chunk, LX)
        src, dst, to = (
            (u.at[part], uz.at[step, part], {"sub": z_down}),
            (u.at[part], ut.at[step, part], {"grp": t_down}),
            (zs.at[part], bz.at[step, part], {"sub": z_up}),
            (ts.at[part], bt.at[step, part], {"grp": t_up}),
        )[kind]
        return pltpu.make_async_remote_copy(
            src_ref=src, dst_ref=dst, send_sem=halo_send.at[step, kind, chunk],
            recv_sem=halo_recv.at[step, kind, chunk], device_id=to, device_id_type=MESH,
        )

    def y_halo(step, kind):
        src, dst = (
            (u.at[pl.ds(0, LX)], uy.at[step]),
            (ys, by.at[step]),
        )[kind]
        return pltpu.make_async_remote_copy(
            src_ref=src, dst_ref=dst, send_sem=y_send.at[step, kind],
            recv_sem=y_recv.at[step, kind], device_id={"sub": other}, device_id_type=MESH,
        )

    def sum_copy(step, stage, d):
        to, buf = partner(stage, d), (rows, cols)[stage]
        return pltpu.make_async_remote_copy(
            src_ref=buf.at[step, 0], dst_ref=buf.at[step, d], send_sem=sum_send.at[step, stage],
            recv_sem=sum_recv.at[step, stage], device_id=to, device_id_type=MESH,
        )

    def begin(l, _):
        start = got_rhs[table[1, l]]
        u[l] = start
        image[l] = start.astype(f32) * (-1.0 / GUESS)
        v[l] = jnp.zeros_like(start)
        res[l] = jnp.zeros((BLK, RHS), f32)
        sol[l] = jnp.zeros((BLK, RHS), f32)
        halo_sum[l] = jnp.zeros((BLK, RHS), f32)
        return 0

    def take_blocks(turn, _):
        d = spread_out(turn)
        who = along_sub(-d)
        block_copy(d, along_sub(d), who).wait()
        for k in range(2):
            for tile in range(3):
                got_op[2 * who + k, :, 128 * tile : 128 * tile + 128] = dense[who, pl.ds((3 * k + tile) * BLK, BLK)]
        last_part = dense[who, pl.ds(6 * BLK, 144)]
        side = last_part[:, BLK:]
        rest = jnp.concatenate([side[:48], side[48:96], side[96:]], axis=1)
        got_op[2 * who, :, 384:] = last_part[:BLK, :BLK]
        got_op[2 * who + 1, :, 384:] = jnp.concatenate([last_part[BLK:, :BLK], rest], axis=0)
        flip(who)
        return 0

    def send_ahead(step, chunk):
        halo(step, 0, chunk).start()
        halo(step, 1, chunk).start()
        if chunk == 0:
            y_halo(step, 0).start()

    def send_behind(step, chunk):
        def far_terms(l, _):
            terms = jnp.dot(flipped[table[1, l], 2 * BLK :], u[l], preferred_element_type=f32)
            zs[l] = terms[:BLK].astype(bf16)
            ts[l] = terms[BLK:].astype(bf16)
            return 0

        def y_terms(x, _):
            l = SITES - LX + x
            terms = jnp.dot(flipped[table[1, l], BLK : 2 * BLK], u[l], preferred_element_type=f32)
            ys[x] = terms.astype(bf16)
            return 0

        lax.fori_loop(LX * chunk, LX * chunk + LX, far_terms, 0, unroll=8)
        halo(step, 2, chunk).start()
        halo(step, 3, chunk).start()
        if chunk == LY - 1:
            lax.fori_loop(0, LX, y_terms, 0, unroll=8)
            y_halo(step, 1).start()

    def start_sums(step, stage):
        for d in range(1, 16):
            sum_copy(step, stage, d).start()

    def finish_sums(step, stage):
        buf = (rows, cols)[stage]
        others = buf.at[step, pl.ds(1, 15)]
        pltpu.make_async_remote_copy(
            src_ref=others, dst_ref=others, send_sem=sum_send.at[step, stage],
            recv_sem=sum_recv.at[step, stage], device_id={"sub": along_sub(1)}, device_id_type=MESH,
        ).wait()
        return jnp.sum(buf[step], axis=0)

    def send_rest(step):
        for chunk in range(FIRST, LY):
            send_ahead(step, chunk)
            send_behind(step, chunk)

    def early_copy(kind):
        part = pl.ds(0, EARLY)
        return pltpu.make_async_remote_copy(
            src_ref=(home.at[0, part], v.at[part], u.at[part])[kind], dst_ref=early.at[kind],
            send_sem=early_send.at[kind], recv_sem=early_recv.at[kind],
            device_id={"sub": here}, device_id_type=MESH,
        )

    def set_alpha(step, more):
        cols[step, 0] = finish_sums(step, 0)
        start_sums(step, 1)
        if more:
            send_rest(step + 1)
        else:

            @pl.when(here != sub)
            def _():
                early_copy(2).start()

        both = finish_sums(step, 1)
        alpha[...] = both[0:1] / both[1:2]

    lax.fori_loop(0, SITES, begin, 0, unroll=4)
    alpha[...] = jnp.full_like(alpha, GUESS)
    y_halo(0, 0).start()
    for chunk in range(LY):
        halo(0, 1, chunk).start()
    lax.fori_loop(1, 16, take_blocks, 0)
    for chunk in range(LY):
        halo(0, 0, chunk).start()
        send_behind(0, chunk)

    def one_step(step, _):
        @pl.when(step > 0)
        def _():
            set_alpha(step - 1, True)

        def update(l, _):
            sol[l] = sol[l] + alpha[...] * v[l].astype(f32)
            new = res[l] - alpha[...] * image[l]
            res[l] = new
            v[l] = new.astype(bf16)
            return 0

        def behind(l, _):
            terms = jnp.dot(flipped[table[1, l], : 2 * BLK], v[l], preferred_element_type=f32)
            bx[l] = terms[:BLK]
            byl[l] = terms[BLK:]
            return 0

        lax.fori_loop(0, SITES, update, 0, unroll=8)
        lax.fori_loop(0, SITES, behind, 0, unroll=8)

        def near(chunk):
            def site(x, _):
                l = LX * chunk + x
                this = v[l]
                stack = [this, v[LX * chunk + lax.rem(x + 1, LX)]]
                if chunk < LY - 1:
                    stack.append(v[l + LX])
                total = jnp.dot(
                    got_op[table[1, l], :, : len(stack) * BLK], jnp.concatenate(stack, axis=0), preferred_element_type=f32
                )
                total = total + 4.0 * this.astype(f32) + bx[LX * chunk + lax.rem(x + LX - 1, LX)]
                if chunk > 0:
                    total = total + byl[l - LX]
                image[l] = total
                return 0

            lax.fori_loop(0, LX, site, 0, unroll=8)

        for chunk in range(LY):
            near(chunk)

        def far(chunk, carry):
            first = CUT // 2 if chunk == LY - 1 else CUT

            def site(x, carry):
                cross, power = carry
                l = LX * chunk + x
                stack = [uz[step, l], ut[step, l]]
                if chunk == LY - 1:
                    stack = [uy[step, x]] + stack
                stack = [jnp.zeros((WIDE - first - len(stack) * BLK, RHS), bf16)] + stack
                term = jnp.dot(
                    got_op[table[1, l], :, first:], jnp.concatenate(stack, axis=0), preferred_element_type=f32
                )
                term = term + bz[step, l].astype(f32) + bt[step, l].astype(f32)
                if chunk == 0:
                    term = term + by[step, x].astype(f32)
                held = halo_sum[l]
                outer = held + alpha[...] / GUESS * (term - held)
                halo_sum[l] = outer
                total = image[l] + outer
                image[l] = total
                old = res[l]
                u[l] = (old - GUESS * total).astype(bf16)
                cross = cross + jnp.sum((total * old).reshape(BLK // 8, 8, RHS), axis=0)
                power = power + jnp.sum((total * total).reshape(BLK // 8, 8, RHS), axis=0)
                return cross, power

            return lax.fori_loop(0, LX, site, carry, unroll=8)

        y_halo(step, 0).wait()
        y_halo(step, 1).wait()
        carry = (jnp.zeros((8, RHS), f32), jnp.zeros((8, RHS), f32))
        for chunk in range(LY):
            for kind in range(4):
                halo(step, kind, chunk).wait()
            carry = far(chunk, carry)
        rows[step, 0] = jnp.concatenate([jnp.sum(c, axis=0, keepdims=True) for c in carry], axis=0)
        start_sums(step, 0)

        @pl.when(step < STEPS - 1)
        def _():
            for chunk in range(FIRST):
                send_ahead(step + 1, chunk)
                send_behind(step + 1, chunk)

        @pl.when((step == STEPS - 1) & (here != sub))
        def _():
            for l in range(EARLY):
                home[0, l] = sol[l].astype(bf16)
            early_copy(0).start()
            early_copy(1).start()

        return 0

    lax.fori_loop(0, STEPS, one_step, 0)
    set_alpha(STEPS - 1, False)

    def last(l, _):
        home[0, l] = (sol[l] + alpha[...] * v[l].astype(f32)).astype(bf16)
        home[1, l] = (res[l] - alpha[...] * image[l]).astype(bf16)
        return 0

    column, height = sub // 8, sub % 8
    source_height = 4 + 3 * column
    far_owner = 8 - 5 * column
    outs = (sol_out, res_out)

    def beside(up):
        return 8 * column + lax.rem(source_height + (2 if up else 6), 8)

    is_source = height == source_height
    is_stop = [sub == beside(False), sub == beside(True)]

    def span(chunk):
        return (EARLY, LX - EARLY) if chunk == 0 else (LX * chunk, LX)

    def home_copy(kind, chunk):
        part = pl.ds(*span(chunk))
        return pltpu.make_async_remote_copy(
            src_ref=home.at[kind, part], dst_ref=outs[kind].at[part],
            send_sem=home_send.at[kind, chunk], recv_sem=home_recv.at[kind, chunk],
            device_id={"sub": here}, device_id_type=MESH,
        )

    def first_leg(kind, chunk):
        return pltpu.make_async_remote_copy(
            src_ref=home.at[kind, pl.ds(*span(chunk))], dst_ref=stop.at[kind, chunk // 2, pl.ds(0, span(chunk)[1])],
            send_sem=home_send.at[kind, chunk], recv_sem=stop_recv.at[kind, chunk // 2],
            device_id={"sub": beside(chunk % 2 == 1)}, device_id_type=MESH,
        )

    def second_leg(kind, chunk):
        return pltpu.make_async_remote_copy(
            src_ref=stop.at[kind, chunk // 2, pl.ds(0, span(chunk)[1])], dst_ref=outs[kind].at[pl.ds(*span(chunk))],
            send_sem=stop_send.at[kind, chunk // 2], recv_sem=home_recv.at[kind, chunk],
            device_id={"sub": far_owner}, device_id_type=MESH,
        )

    for chunk in range(LY):
        lax.fori_loop(span(chunk)[0], sum(span(chunk)), last, 0, unroll=2)

        @pl.when(is_source)
        def _():
            for kind in range(2):
                first_leg(kind, chunk).start()

        @pl.when((here != sub) & (height != source_height))
        def _():
            for kind in range(2):
                home_copy(kind, chunk).start()

    for up in range(2):

        @pl.when(is_stop[up])
        def _():
            for chunk in (up, up + 2):
                for kind in range(2):
                    first_leg(kind, chunk).wait_recv()
                    second_leg(kind, chunk).start()

    @pl.when(here == sub)
    def _():
        lax.fori_loop(0, EARLY, last, 0, unroll=2)

        def keep(l, _):
            sol_out[l] = home[0, l]
            res_out[l] = home[1, l]
            return 0

        lax.fori_loop(0, SITES, keep, 0)

    @pl.when(here != sub)
    def _():
        for kind in range(3):
            early_copy(kind).wait()
        for l in range(EARLY):
            old = early[1, l].astype(f32)
            sol_out[l] = (early[0, l].astype(f32) + alpha[...] * old).astype(bf16)
            res_out[l] = (old + alpha[...] / GUESS * (early[2, l].astype(f32) - old)).astype(bf16)
        for chunk in range(LY):
            for kind in range(2):
                home_copy(kind, chunk).wait()

    for up in range(2):

        @pl.when(is_stop[up])
        def _():
            for chunk in (up, up + 2):
                for kind in range(2):
                    second_leg(kind, chunk).wait_send()


def on_device(operator_fine, rhs_fine, fine_site):
    f32, bf16 = jnp.float32, jnp.bfloat16
    vector = (SITES, BLK, RHS)
    whole = pl.BlockSpec(memory_space=pltpu.VMEM)
    dma = pltpu.SemaphoreType.DMA
    sol, res = pl.pallas_call(
        kernel,
        out_shape=(pltpu.VMEM(vector, bf16), pltpu.VMEM(vector, bf16)),
        in_specs=[whole, pl.BlockSpec(memory_space=pl.ANY), pl.BlockSpec(memory_space=pl.ANY)],
        out_specs=(whole, whole),
        scratch_shapes=[
            pltpu.VMEM((SITES, BLK, WIDE), bf16),
            pltpu.VMEM(vector, bf16),
            pltpu.VMEM((2, 128), jnp.int32),
            pltpu.SMEM((2, 128), jnp.int32),
            pltpu.VMEM((N_SUB, 720, 128), bf16),
            pltpu.VMEM((N_SUB, 720, 128), bf16),
            pltpu.VMEM(vector, bf16),
            pltpu.VMEM((SITES, BLK, WIDE), bf16),
            pltpu.VMEM(vector, bf16),
            pltpu.VMEM((SITES, 4 * BLK, BLK), bf16),
            pltpu.VMEM(vector, bf16),
            pltpu.VMEM((STEPS,) + vector, bf16),
            pltpu.VMEM((STEPS,) + vector, bf16),
            pltpu.VMEM((STEPS, LX, BLK, RHS), bf16),
            pltpu.VMEM(vector, bf16),
            pltpu.VMEM(vector, bf16),
            pltpu.VMEM((LX, BLK, RHS), bf16),
            pltpu.VMEM((STEPS,) + vector, bf16),
            pltpu.VMEM((STEPS,) + vector, bf16),
            pltpu.VMEM((STEPS, LX, BLK, RHS), bf16),
            pltpu.VMEM(vector, bf16),
            pltpu.VMEM(vector, f32),
            pltpu.VMEM(vector, f32),
            pltpu.VMEM(vector, f32),
            pltpu.VMEM(vector, f32),
            pltpu.VMEM(vector, f32),
            pltpu.VMEM(vector, f32),
            pltpu.VMEM((2,) + vector, bf16),
            pltpu.VMEM((2, 2, LX, BLK, RHS), bf16),
            pltpu.VMEM((3, EARLY, BLK, RHS), bf16),
            pltpu.VMEM((1, RHS), f32),
            pltpu.VMEM((STEPS, 16, 2, RHS), f32),
            pltpu.VMEM((STEPS, 16, 2, RHS), f32),
            dma((16,)), dma((16,)), dma((16,)), dma((16,)),
            dma((STEPS, 4, LY)), dma((STEPS, 4, LY)),
            dma((STEPS, 2)), dma((STEPS, 2)),
            dma((STEPS, 2)), dma((STEPS, 2)), dma((2, LY)), dma((2, LY)), dma((2, 2)), dma((2, 2)),
            dma((3,)), dma((3,)), dma((3,)),
        ],
        compiler_params=pltpu.CompilerParams(
            collective_id=0, has_side_effects=True, vmem_limit_bytes=60 * 2**20
        ),
    )(fine_site.reshape(4, 128), operator_fine, rhs_fine)
    return sol.astype(f32), res.astype(f32)


def solution(mesh):
    in_specs = (P(("grp", "sub"), None, None), P(("grp", "sub"), None, None), P("grp"))
    out_specs = (P(("grp", "sub"), None, None), P(("grp", "sub"), None, None))
    return jax.shard_map(
        on_device, mesh=mesh, in_specs=in_specs, out_specs=out_specs, check_vma=False
    )
```
